512 devices in a mesh: mirror: 2 (over core), slab: 256 (over y, z, x).
Axes of the slice: x: 4, y: 4, z: 16, core: 2. Of those that a mesh axis runs over, the one named last changes fastest.
Arguments:
- density: float32 [1024, 8, 128], P('slab'), may hold values from 0.2 to 1
- load_mask: int32 [2, 1024, 8, 128], P('mirror', 'slab'), may hold values 0 or 1
- fixed_mask: int32 [2, 1024, 8, 128], P('mirror', 'slab'), may hold values 0 or 1
- sweeps: int32 [2], replicated, may hold values from 1 to 4, as said below
Outputs:
- displacement: float32 [2, 3, 1024, 8, 128], P('mirror', None, 'slab')
- residual: float32 [2, 3, 1024, 8, 128], P('mirror', None, 'slab')
- sensitivity: float32 [1024, 8, 128], P('slab')
The draws below stay inside these ranges and needn't reach their ends.
Inputs may be any that keep to these rules, and one draw needn't show every extreme that they name: `sweeps`: one of the two counts is 4.
All inputs are finite; a program needn't handle non-finite values. No bound on the sum of `load_mask` or of `fixed_mask` on one device may be relied on, other than what follows from the above.
Results may differ from the reference program's by a relative error of at most 0.0003.
Values sent between devices are 32-bit elements; how exact they have to be, the bound alone decides.
No kernel may reach another device: no remote copies, remote signals or barrier semaphores. Data moves between devices by JAX's collectives and lax.ppermute only.
A program may use at most 64 MiB of HBM per device.

```python
import jax
import jax.numpy as jnp
import numpy as np
from jax import lax

X = 128
Y = 8
SWEEPS = 4
Z = 1024


def draw_sweeps(key, part):
    key = jax.random.fold_in(key, 7)
    picked = jax.random.randint(jax.random.fold_in(key, 1), (), 0, 7)
    leading = jnp.where(picked < 4, 4, picked - 3)
    trailing = jnp.where(picked < 4, picked + 1, 4)
    return jnp.stack([leading, trailing]).astype(jnp.int32)


def touch_ends(values, rng, smallest, top_value):
    extent = values.shape
    index_at = [jax.random.randint(jax.random.fold_in(rng, axis), (), 0, extent[axis]) for axis in range(len(extent))]
    values = values.at[tuple(index_at)].set(smallest)
    longest = extent.index(max(extent))
    index_at[longest] = (index_at[longest] + 1) % extent[longest]
    return values.at[tuple(index_at)].set(top_value)


def block_scale(stream_key, shape, cuts, smallest, high):
    def one(axis_at, blocks):
        draws = jax.random.uniform(jax.random.fold_in(jax.random.fold_in(stream_key, 6), axis_at), (blocks,), jnp.float32, smallest / len(cuts), high / len(cuts))
        return jnp.repeat(jnp.exp(draws), shape[axis_at] // blocks).reshape((-1,) + (1,) * (len(shape) - axis_at - 1))

    level = one(*cuts[0])
    for cut in cuts[1:]:
        level = level * one(*cut)
    return level


def setup_inputs(seed: int = 0) -> dict:
    key_list = jax.random.split(jax.random.key(seed), 5)
    return {
        "density": jnp.clip(0.2 + 0.8 * jax.random.uniform(key_list[0], (Z, Y, X), jnp.float32) ** block_scale(key_list[0], (Z, Y, X), ((0, 256),), -0.2, 0.2), 0.2, 1.0),
        "load_mask": touch_ends((jax.random.randint(key_list[1], (2, Z, Y, X), 0, 16) < 1).astype(jnp.int32), jax.random.fold_in(key_list[1], 1), 0, 1),
        "fixed_mask": touch_ends((jax.random.randint(key_list[2], (2, Z, Y, X), 0, 8) < 1).astype(jnp.int32), jax.random.fold_in(key_list[2], 1), 0, 1),
        "sweeps": draw_sweeps(jax.random.fold_in(key_list[4], 71), 0),
    }


MODULUS_FLOOR = 0.001
EIG_LOWER = 0.05
EIG_UPPER = 1.0

def element_matrix():
    poisson = 0.3
    lame_first = poisson / ((1.0 + poisson) * (1.0 - 2.0 * poisson))
    shear_modulus = 0.5 / (1.0 + poisson)
    elastic = np.zeros((6, 6))
    elastic[:3, :3] = lame_first
    for i in range(3):
        elastic[i, i] += 2.0 * shear_modulus
        elastic[i + 3, i + 3] = shear_modulus
    points = [0.5 - 0.5 / np.sqrt(3.0), 0.5 + 0.5 / np.sqrt(3.0)]
    stiffness = np.zeros((24, 24))
    for p in points:
        for q in points:
            for s in points:
                strain = np.zeros((6, 24))
                for corner in range(8):
                    z_bit, y_bit, x_bit = (corner // 4, corner // 2 % 2, corner % 2)
                    weight_z = p if z_bit else 1.0 - p
                    weight_y = q if y_bit else 1.0 - q
                    weight_x = s if x_bit else 1.0 - s
                    slope_z = 1.0 if z_bit else -1.0
                    slope_y = 1.0 if y_bit else -1.0
                    slope_x = 1.0 if x_bit else -1.0
                    grad_x = slope_x * weight_y * weight_z
                    grad_y = weight_x * slope_y * weight_z
                    grad_z = weight_x * weight_y * slope_z
                    c = 3 * corner
                    strain[0, c] = grad_x
                    strain[1, c + 1] = grad_y
                    strain[2, c + 2] = grad_z
                    strain[3, c] = grad_y
                    strain[3, c + 1] = grad_x
                    strain[4, c + 1] = grad_z
                    strain[4, c + 2] = grad_y
                    strain[5, c] = grad_z
                    strain[5, c + 2] = grad_x
                stiffness += strain.T @ elastic @ strain / 8.0
    return stiffness

def element_terms(extended, stiffness):
    planes, rows_y, cols_x = (extended.shape[1] - 1, extended.shape[2] - 1, extended.shape[3] - 1)
    blocks = []
    for corner in range(8):
        z_bit, y_bit, x_bit = (corner // 4, corner // 2 % 2, corner % 2)
        blocks.append(extended[:, z_bit:z_bit + planes, y_bit:y_bit + rows_y, x_bit:x_bit + cols_x])
    local_dofs = jnp.concatenate(blocks, axis=0)
    forces = jnp.einsum('ij,jabc->iabc', stiffness, local_dofs, precision=lax.Precision.HIGHEST)
    return (local_dofs, forces)

def spread_corners(forces):
    summed = None
    for corner in range(8):
        z_bit, y_bit, x_bit = (corner // 4, corner // 2 % 2, corner % 2)
        padded = jnp.pad(forces[3 * corner:3 * corner + 3], ((0, 0), (z_bit, 1 - z_bit), (y_bit, 1 - y_bit), (x_bit, 1 - x_bit)))
        summed = padded if summed is None else summed + padded
    return summed

def operate(vector, modulus, stiffness, free_mask):
    masked = free_mask * vector
    extended = jnp.pad(masked, ((0, 0), (0, 1), (0, 1), (0, 1)))
    _, forces = element_terms(extended, stiffness)
    spread = spread_corners(modulus[None] * forces)
    planes, rows_y, cols_x = modulus.shape
    return free_mask * spread[:, :planes, :rows_y, :cols_x] + (1.0 - free_mask) * vector

def l1_diagonal(modulus, stiffness, free_mask):
    row_abs = lax.optimization_barrier(jnp.sum(jnp.abs(stiffness), axis=1))
    spread = spread_corners(row_abs[:, None, None, None] * modulus[None])
    planes, rows_y, cols_x = modulus.shape
    return free_mask * spread[:, :planes, :rows_y, :cols_x] + (1.0 - free_mask)

def chebyshev(operator_fn, scaling, target, sweep_count):
    centre_eig = 0.5 * (EIG_UPPER + EIG_LOWER)
    half_width = 0.5 * (EIG_UPPER - EIG_LOWER)
    ratio_eig = centre_eig / half_width
    rho_now = 1.0 / ratio_eig
    update = target / (scaling * centre_eig)
    iterate = update
    for k in range(1, SWEEPS):
        defect = target - operator_fn(iterate)
        rho_next = 1.0 / (2.0 * ratio_eig - rho_now)
        update_next = rho_next * rho_now * update + 2.0 * rho_next / half_width * defect / scaling
        taken = k < sweep_count
        iterate = jnp.where(taken, iterate + update_next, iterate)
        update = jnp.where(taken, update_next, update)
        rho_now = rho_next
    return iterate

def restrict_sum(vector):
    comps, planes, rows_y, cols_x = vector.shape
    grouped = vector.reshape(comps, planes // 4, 4, rows_y // 4, 4, cols_x // 4, 4)
    return lax.optimization_barrier(jnp.sum(grouped, axis=(2, 4, 6)))

def coarse_modulus(modulus):
    planes, rows_y, cols_x = modulus.shape
    grouped = modulus.reshape(planes // 4, 4, rows_y // 4, 4, cols_x // 4, 4)
    return lax.optimization_barrier(jnp.mean(grouped, axis=(1, 3, 5)))

def prolong_copy(vector):
    return jnp.repeat(jnp.repeat(jnp.repeat(vector, 4, axis=1), 4, axis=2), 4, axis=3)

def reference(density, load_mask, fixed_mask, sweeps):
    stiffness = jnp.asarray(element_matrix(), jnp.float32)
    modulus_half = MODULUS_FLOOR + density ** 3 * (1.0 - MODULUS_FLOOR)
    modulus = jnp.concatenate([modulus_half, modulus_half[..., ::-1]], axis=-1)
    density_full = jnp.concatenate([density, density[..., ::-1]], axis=-1)
    free_mask = jnp.concatenate([1 - fixed_mask[0], 1 - fixed_mask[1]], axis=-1).astype(jnp.float32)[None]
    loads = jnp.concatenate([load_mask[0], load_mask[1]], axis=-1).astype(jnp.float32)[None]
    direction = jnp.array([0.4, -0.3, -1.0], jnp.float32)[:, None, None, None]
    right = free_mask * loads * direction

    def fine_op(vector):
        return operate(vector, modulus, stiffness, free_mask)
    fine_scale = l1_diagonal(modulus, stiffness, free_mask)
    modulus_low = coarse_modulus(modulus)
    coarse_free = jnp.ones((1,) + modulus_low.shape, jnp.float32)
    coarse_stiff = 4.0 * stiffness

    def coarse_op(vector):
        return operate(vector, modulus_low, coarse_stiff, coarse_free)
    coarse_scale = l1_diagonal(modulus_low, coarse_stiff, coarse_free)
    smooth = chebyshev(fine_op, fine_scale, right, sweeps[0])
    leftover = right - fine_op(smooth)
    coarse_sol = chebyshev(coarse_op, coarse_scale, restrict_sum(leftover), sweeps[1])
    precond = smooth + free_mask * prolong_copy(coarse_sol)
    residual_dot = jnp.sum(right * precond)
    image = fine_op(precond)
    curvature = jnp.sum(precond * image)
    alpha = residual_dot / curvature
    moved = alpha * precond
    left_over = right - alpha * image
    extended = jnp.pad(moved, ((0, 0), (0, 1), (0, 1), (0, 1)))
    local_dofs, forces = element_terms(extended, stiffness)
    energy = lax.optimization_barrier(jnp.sum(local_dofs * forces, axis=0))
    slope = -3.0 * density_full ** 2 * (1.0 - MODULUS_FLOOR) * energy
    sensitivity = slope[..., :X] + slope[..., X:][..., ::-1]
    displacement = jnp.stack([moved[..., :X], moved[..., X:]])
    residual = jnp.stack([left_over[..., :X], left_over[..., X:]])
    return (displacement, residual, sensitivity)
```

```python
import functools

import jax
import jax.numpy as jnp
import numpy as np
from jax import lax
from jax.experimental import pallas as pl
from jax.experimental.pallas import tpu as pltpu
from jax.sharding import Mesh
from jax.sharding import PartitionSpec as P

SWEEPS = 4
MODULUS_FLOOR = 0.001
EIG_LOWER = 0.05
EIG_UPPER = 1.0
CENTRE = 0.5 * (EIG_UPPER + EIG_LOWER)
HALF_WIDTH = 0.5 * (EIG_UPPER - EIG_LOWER)
DIRECTION = (0.4, -0.3, -1.0)
SLAB = ("y", "z", "x")
ROWS = 8
COLS = 256
OWN = 4


def element_matrix():
    poisson = 0.3
    lame_first = poisson / ((1.0 + poisson) * (1.0 - 2.0 * poisson))
    shear_modulus = 0.5 / (1.0 + poisson)
    elastic = np.zeros((6, 6))
    elastic[:3, :3] = lame_first
    for i in range(3):
        elastic[i, i] += 2.0 * shear_modulus
        elastic[i + 3, i + 3] = shear_modulus
    points = [0.5 - 0.5 / np.sqrt(3.0), 0.5 + 0.5 / np.sqrt(3.0)]
    stiffness = np.zeros((24, 24))
    for p in points:
        for q in points:
            for s in points:
                strain = np.zeros((6, 24))
                for corner in range(8):
                    z_bit, y_bit, x_bit = (corner // 4, corner // 2 % 2, corner % 2)
                    weight_z = p if z_bit else 1.0 - p
                    weight_y = q if y_bit else 1.0 - q
                    weight_x = s if x_bit else 1.0 - s
                    slope_z = 1.0 if z_bit else -1.0
                    slope_y = 1.0 if y_bit else -1.0
                    slope_x = 1.0 if x_bit else -1.0
                    grad_x = slope_x * weight_y * weight_z
                    grad_y = weight_x * slope_y * weight_z
                    grad_z = weight_x * weight_y * slope_z
                    c = 3 * corner
                    strain[0, c] = grad_x
                    strain[1, c + 1] = grad_y
                    strain[2, c + 2] = grad_z
                    strain[3, c] = grad_y
                    strain[3, c + 1] = grad_x
                    strain[4, c + 1] = grad_z
                    strain[4, c + 2] = grad_y
                    strain[5, c] = grad_z
                    strain[5, c + 2] = grad_x
                stiffness += strain.T @ elastic @ strain / 8.0
    return stiffness


@functools.lru_cache(None)
def mode_matrix():
    one = np.array([[1.0, 1.0], [-1.0, 1.0]])
    signs = np.kron(np.kron(one, one), one)
    spread = np.kron(signs, np.eye(3)) / 8.0
    matrix = spread @ element_matrix() @ spread.T
    table = {}
    for row in range(24):
        entries = [
            ((col // 3, col % 3), float(matrix[row, col]))
            for col in range(24)
            if abs(matrix[row, col]) > 1e-12
        ]
        if entries:
            table[(row // 3, row % 3)] = entries
    return table


@functools.lru_cache(None)
def row_total():
    totals = np.abs(element_matrix()).sum(axis=1)
    assert np.allclose(totals, totals[0], rtol=1e-12)
    return float(totals[0])


def chebyshev_factors():
    ratio = CENTRE / HALF_WIDTH
    rho = 1.0 / ratio
    factors = []
    for _ in range(1, SWEEPS):
        rho_next = 1.0 / (2.0 * ratio - rho)
        factors.append((rho_next * rho, 2.0 * rho_next / HALF_WIDTH))
        rho = rho_next
    return factors


class Plane:
    def __init__(self, step):
        lane = lax.broadcasted_iota(jnp.int32, (ROWS, COLS), 1)
        row = lax.broadcasted_iota(jnp.int32, (ROWS, COLS), 0)
        self.step = step
        self.lane_not_last = lane < COLS - step
        self.lane_not_first = lane >= step
        self.row_not_last = row < ROWS - step
        self.row_not_first = row >= step

    def next_x(self, v):
        return jnp.where(self.lane_not_last, pltpu.roll(v, COLS - self.step, 1), 0.0)

    def prev_x(self, v):
        return jnp.where(self.lane_not_first, pltpu.roll(v, self.step, 1), 0.0)

    def next_y(self, v):
        return jnp.where(self.row_not_last, pltpu.roll(v, ROWS - self.step, 0), 0.0)

    def prev_y(self, v):
        return jnp.where(self.row_not_first, pltpu.roll(v, self.step, 0), 0.0)

    def corner_sum(self, v):
        v = v + self.prev_x(v)
        return v + self.prev_y(v)

    def forward(self, comps):
        modes = [[None] * 3 for _ in range(4)]
        for c, v in enumerate(comps):
            ahead = self.next_x(v)
            for x_bit, w in enumerate((ahead + v, ahead - v)):
                above = self.next_y(w)
                modes[x_bit][c] = above + w
                modes[2 + x_bit][c] = above - w
        return modes

    def backward(self, modes):
        comps = []
        for c in range(3):
            along = []
            for x_bit in range(2):
                total, change = modes[x_bit][c], modes[2 + x_bit][c]
                along.append((total - change) + self.prev_y(total + change))
            comps.append((along[0] - along[1]) + self.prev_x(along[0] + along[1]))
        return comps

    def element(self, low, high, modulus, scale, with_energy=False):
        modes = {}
        for m in range(4):
            for c in range(3):
                if m > 0:
                    modes[(m, c)] = high[m][c] + low[m][c]
                modes[(4 + m, c)] = high[m][c] - low[m][c]
        forces = {}
        for row, entries in mode_matrix().items():
            total = None
            for col, entry in entries:
                term = modes[col] * np.float32(entry * scale)
                total = term if total is None else total + term
            forces[row] = total
        energy = None
        if with_energy:
            for row, force in forces.items():
                term = modes[row] * force
                energy = term if energy is None else energy + term
        on_low = [[None] * 3 for _ in range(4)]
        on_high = [[None] * 3 for _ in range(4)]
        for m in range(4):
            for c in range(3):
                change = modulus * forces[(4 + m, c)]
                if m > 0:
                    total = modulus * forces[(m, c)]
                    on_low[m][c] = total - change
                    on_high[m][c] = total + change
                else:
                    on_low[m][c] = -change
                    on_high[m][c] = change
        return on_low, on_high, energy


def apply_planes(plane, first, last, load, modulus_at, scale, consume, with_energy=False):
    def flat(modes):
        return tuple(v for mode in modes for v in mode)

    def nested(values):
        return [[values[3 * m + c] for c in range(3)] for m in range(4)]

    def body(p, carry):
        low, pending = nested(carry[:12]), nested(carry[12:])
        high = plane.forward(load(p + 1))
        on_low, on_high, energy = plane.element(low, high, modulus_at(p), scale, with_energy)
        total = [[pending[m][c] + on_low[m][c] for c in range(3)] for m in range(4)]
        consume(p, plane.backward(total), energy)
        return flat(high) + flat(on_high)

    start = flat(plane.forward(load(first - 1)))
    zeros = tuple(jnp.zeros((ROWS, COLS), jnp.float32) for _ in range(12))
    lax.fori_loop(first - 1, last + 1, body, start + zeros)


class Groups:
    def __init__(self):
        lane = lax.broadcasted_iota(jnp.int32, (ROWS, COLS), 1)
        row = lax.broadcasted_iota(jnp.int32, (ROWS, COLS), 0)
        self.lane_in, self.row_in = lane % 4, row % 4
        self.lane_bits = [lane % 2 == 1, lane // 2 % 2 == 1]
        self.row_bits = [row % 2 == 1, row // 2 % 2 == 1]

    def over_rows(self, v):
        for bit in range(2):
            by = 1 << bit
            v = v + jnp.where(self.row_bits[bit], pltpu.roll(v, by, 0), pltpu.roll(v, ROWS - by, 0))
        return v

    def over_lanes(self, v):
        for bit in range(2):
            by = 1 << bit
            v = v + jnp.where(self.lane_bits[bit], pltpu.roll(v, by, 1), pltpu.roll(v, COLS - by, 1))
        return v

    def both(self, v):
        return self.over_lanes(self.over_rows(v))


def modulus_of(density):
    return MODULUS_FLOOR + density * density * density * (1.0 - MODULUS_FLOOR)


def smooth_kernel(slabs, info, own, below, above, edge, smooth, coarse, mod, x, d, w, right, free, left):
    plane, groups = Plane(1), Groups()
    slab, sweep_count = info[0], info[2]
    has_below = (slab > 0).astype(jnp.float32)
    has_edge = (slab > 1).astype(jnp.float32)
    has_above = (slab < slabs - 1).astype(jnp.float32)

    mod[0] = modulus_of(edge[0]) * has_edge
    for source, at, inside in ((below, 0, has_below), (own, 4, None), (above, 8, has_above)):
        for k in range(OWN):
            value = modulus_of(source[0, k])
            mod[1 + at + k] = value if inside is None else value * inside
            open_node = 1.0 - source[2, k]
            free[at + k] = open_node if inside is None else open_node * inside

    def prepare(q, carry):
        summed = plane.corner_sum(mod[q + 1])
        scaling = np.float32(row_total()) * (carry + summed)
        f = free[q]
        scaling = jnp.where(f > 0.0, scaling, 1.0)
        inverse = 1.0 / scaling
        w[q] = inverse
        return summed

    lax.fori_loop(0, 12, prepare, plane.corner_sum(mod[0]))
    for source, at in ((below, 0), (own, 4), (above, 8)):
        for k in range(OWN):
            loaded = free[at + k] * source[1, k]
            start = loaded * (w[at + k] * np.float32(1.0 / CENTRE))
            right[at + k] = loaded
            for c in range(3):
                x[c, at + k] = start * np.float32(DIRECTION[c])
                d[c, at + k] = start * np.float32(DIRECTION[c])

    def load(q):
        f = free[q]
        return [f * x[c, q] for c in range(3)]

    def modulus_at(q):
        return mod[q + 1]

    for k, (keep, add) in enumerate(chebyshev_factors(), 1):

        @pl.when(k < sweep_count)
        def _(k=k, keep=keep, add=add):
            def consume(q, forces, _energy):
                f, weight = free[q], w[q] * np.float32(add)
                is_free = f > 0.0
                loaded = right[q]
                for c in range(3):
                    now = x[c, q]
                    image = jnp.where(is_free, forces[c], now)
                    defect = loaded * np.float32(DIRECTION[c]) - image
                    update = np.float32(keep) * d[c, q] + weight * defect
                    d[c, q] = update
                    x[c, q] = now + update

            apply_planes(plane, k, 11 - k, load, modulus_at, 1.0, consume)

    def consume_left(q, forces, _energy):
        is_free = free[q] > 0.0
        for c in range(3):
            image = jnp.where(is_free, forces[c], x[c, q])
            left[c, q - 3] = right[q] * np.float32(DIRECTION[c]) - image

    apply_planes(plane, 4, 7, load, modulus_at, 1.0, consume_left)

    for c in range(3):
        for k in range(6):
            smooth[c, k] = x[c, k + 3]
    fields = [groups.both((left[c, 1] + left[c, 2]) + (left[c, 3] + left[c, 4])) for c in range(3)]
    here = groups.both((mod[5] + mod[6]) + (mod[7] + mod[8])) * np.float32(1.0 / 64.0)
    under = groups.both((mod[1] + mod[2]) + (mod[3] + mod[4])) * np.float32(1.0 / 64.0)
    packed = jnp.where(groups.lane_in == 0, here, under)
    for c in range(3):
        packed = jnp.where(groups.row_in == c, fields[c], packed)
    coarse[...] = packed


def correct_kernel(
    slabs, info, own, below, above, smooth, gathered, moved, image, slope, sums, window, mod, x, d, w, target, p, free, img, energy
):
    coarse_plane, plane, groups = Plane(4), Plane(1), Groups()
    slab, mirror, sweep_count = info[0], info[1], info[3]
    offset = slab % 4
    for k in range(4):
        window[k] = gathered[k, ROWS : 2 * ROWS]
        window[4 + k] = gathered[k, :ROWS]
        window[8 + k] = gathered[4 + k, ROWS : 2 * ROWS]

    is_here = (groups.row_in == 3) & (groups.lane_in == 0)
    is_under = (groups.row_in == 3) & (groups.lane_in == 1)

    def unpack(q, carry):
        packed = window[offset + q]
        for c in range(3):
            target[c, q] = groups.over_rows(jnp.where(groups.row_in == c, packed, 0.0))
        mod[q + 1] = groups.both(jnp.where(is_here, packed, 0.0))
        return carry

    lax.fori_loop(0, 9, unpack, 0)
    mod[0] = groups.both(jnp.where(is_under, window[offset], 0.0))

    def prepare(q, carry):
        summed = coarse_plane.corner_sum(mod[q + 1])
        scaling = np.float32(4.0 * row_total()) * (carry + summed)
        at = slab - 4 + q
        inside = ((at >= 0) & (at < slabs)).astype(jnp.float32)
        inverse = inside / jnp.where(scaling > 0.0, scaling, 1.0)
        w[q] = inverse
        for c in range(3):
            start = target[c, q] * (inverse * np.float32(1.0 / CENTRE))
            x[c, q] = start
            d[c, q] = start
        return summed

    lax.fori_loop(0, 9, prepare, coarse_plane.corner_sum(mod[0]))

    for k, (keep, add) in enumerate(chebyshev_factors(), 1):

        @pl.when(k < sweep_count)
        def _(k=k, keep=keep, add=add):
            def consume(q, forces, _energy):
                weight = w[q] * np.float32(add)
                for c in range(3):
                    update = np.float32(keep) * d[c, q] + weight * (target[c, q] - forces[c])
                    d[c, q] = update
                    x[c, q] = x[c, q] + update

            apply_planes(
                coarse_plane,
                k,
                8 - k,
                lambda q: [x[c, q] for c in range(3)],
                lambda q: mod[q + 1],
                4.0,
                consume,
            )

    has_below = (slab > 0).astype(jnp.float32)
    has_above = (slab < slabs - 1).astype(jnp.float32)
    for k in range(6):
        source, at, inside, coarse = (
            (below, 3, has_below, 3) if k == 0 else (above, 0, has_above, 5) if k == 5 else (own, k - 1, None, 4)
        )
        open_node = 1.0 - source[2, at]
        if inside is not None:
            open_node = open_node * inside
        free[k] = open_node
        for c in range(3):
            p[c, k] = smooth[c, k] + open_node * x[c, coarse]
        if k < 5:
            value = modulus_of(source[0, at])
            mod[k] = value if inside is None else value * inside

    def consume_image(q, forces, strain):
        is_free = free[q] > 0.0
        for c in range(3):
            img[c, q] = jnp.where(is_free, forces[c], p[c, q])
        energy[q] = strain

    def load_p(q):
        f = free[q]
        return [f * p[c, q] for c in range(3)]

    apply_planes(plane, 1, 4, load_p, lambda q: mod[q], 1.0, consume_image, True)

    first = jnp.zeros((ROWS, COLS), jnp.float32)
    second = jnp.zeros((ROWS, COLS), jnp.float32)
    half = pl.ds(pl.multiple_of(mirror * 128, 128), 128)
    for k in range(OWN):
        loaded = free[k + 1] * own[1, k]
        for c in range(3):
            first = first + (loaded * np.float32(DIRECTION[c])) * p[c, k + 1]
            second = second + p[c, k + 1] * img[c, k + 1]
            moved[c, k] = p[c, k + 1, :, half]
            image[c, k] = img[c, k + 1, :, half]
        density = own[0, k]
        energy[k + 1] = np.float32(-3.0 * (1.0 - MODULUS_FLOOR)) * (density * density) * energy[k + 1]
    flip = (
        lax.broadcasted_iota(jnp.int32, (128, 128), 0) + lax.broadcasted_iota(jnp.int32, (128, 128), 1) == 127
    ).astype(jnp.float32)
    second_half = jnp.concatenate([energy[k + 1, :, 128:] for k in range(OWN)], axis=0)
    turned = jnp.dot(second_half, flip, precision=lax.Precision.HIGHEST, preferred_element_type=jnp.float32)
    for k in range(OWN):
        slope[k] = energy[k + 1, :, :128] + turned[ROWS * k : ROWS * (k + 1)]
    lane = lax.broadcasted_iota(jnp.int32, (1, 128), 1)
    dots = jnp.where(lane == 0, jnp.sum(first), jnp.where(lane == 1, jnp.sum(second), 0.0))
    for k in range(sums.shape[0]):
        sums[k] = dots


def scale_kernel(totals, load, fixed, moved, image, slope, displacement, residual, sensitivity):
    total = totals[0]
    for k in range(1, totals.shape[0]):
        total = total + totals[k]
    lane = lax.broadcasted_iota(jnp.int32, (1, 128), 1)
    residual_dot = jnp.sum(jnp.where(lane == 0, total, 0.0), axis=1, keepdims=True)
    curvature = jnp.sum(jnp.where(lane == 1, total, 0.0), axis=1, keepdims=True)
    alpha = jnp.broadcast_to(residual_dot / curvature, (ROWS, 128))
    for k in range(OWN):
        loaded = ((1 - fixed[0, k]) * load[0, k]).astype(jnp.float32)
        for c in range(3):
            displacement[c, k] = alpha * moved[c, k]
            residual[c, k] = loaded * np.float32(DIRECTION[c]) - alpha * image[c, k]
        sensitivity[k] = alpha * (alpha * slope[k])


def call(kernel, outs, ins, scratch=()):
    vmem = pl.BlockSpec(memory_space=pltpu.VMEM)
    smem = pl.BlockSpec(memory_space=pltpu.SMEM)
    return pl.pallas_call(
        kernel,
        out_shape=[jax.ShapeDtypeStruct(shape, jnp.float32) for shape in outs],
        in_specs=[smem if v.ndim == 1 else vmem for v in ins],
        out_specs=[vmem] * len(outs),
        scratch_shapes=[pltpu.VMEM(shape, jnp.float32) for shape in scratch],
        compiler_params=pltpu.CompilerParams(vmem_limit_bytes=16 * 1024 * 1024),
    )(*ins)


def shifted(array, axis, by):
    length = lax.axis_size(axis)
    pairs = [(i, i + by) for i in range(length) if 0 <= i + by < length]
    return lax.ppermute(array, axis, pairs)


def on_device(density, load_mask, fixed_mask, sweeps):
    slabs = lax.axis_size(SLAB)
    slab, mirror = lax.axis_index(SLAB), lax.axis_index("mirror")
    info = jnp.concatenate([jnp.stack([slab, mirror]).astype(jnp.int32), sweeps])
    plane = (ROWS, COLS)

    masks = lax.all_gather(jnp.concatenate([load_mask, fixed_mask], axis=0), "mirror")
    masks = jnp.concatenate([masks[0], masks[1]], axis=-1).astype(jnp.float32)
    wide = jnp.concatenate([density, density[..., ::-1]], axis=-1)
    own = jnp.concatenate([wide[None], masks], axis=0)
    below = shifted(own, SLAB, 1)
    above = shifted(own, SLAB, -1)
    edge = shifted(wide[OWN - 1 :], SLAB, 2)

    field = (3, 12) + plane
    smooth, coarse = call(
        functools.partial(smooth_kernel, slabs),
        [(3, 6) + plane, plane],
        [info, own, below, above, edge],
        [(13,) + plane, field, field, (12,) + plane, (12,) + plane, (12,) + plane, (3, 5) + plane],
    )

    reach = 4
    pairs = [(i, i + reach) for i in range(slabs - reach)]
    pairs += [(slabs + i + reach, slabs + i) for i in range(slabs - reach)]
    arrived = lax.ppermute(coarse, ("mirror",) + SLAB, pairs)
    sent = jnp.broadcast_to(jnp.concatenate([coarse, arrived], axis=0), (8, 2 * ROWS, COLS))
    gathered = lax.all_to_all(sent, ("mirror", "x"), 0, 0)

    coarse_field = (3, 9) + plane
    group = lax.axis_size(("y", "x"))
    part = (3, OWN, ROWS, 128)
    moved, image, slope, sums = call(
        functools.partial(correct_kernel, slabs),
        [part, part, part[1:], (group, 1, 128)],
        [info, own, below, above, smooth, gathered],
        [
            (12,) + plane,
            (10,) + plane,
            coarse_field,
            coarse_field,
            (9,) + plane,
            coarse_field,
            (3, 6) + plane,
            (6,) + plane,
            (3, 5) + plane,
            (5,) + plane,
        ],
    )
    sums = lax.all_to_all(sums, ("y", "x"), 0, 0)
    length = lax.axis_size("z")
    sums = jnp.broadcast_to(jnp.sum(sums, axis=0), (length, 1, 128))
    sums = lax.all_to_all(sums, "z", 0, 0)
    displacement, residual, sensitivity = call(
        scale_kernel, [part, part, part[1:]], [sums, load_mask, fixed_mask, moved, image, slope]
    )
    return displacement[None], residual[None], sensitivity


def solution(mesh):
    slabs = mesh.shape["slab"]
    ways = 4
    deep = min(16, slabs // ways)
    split = Mesh(mesh.devices.reshape(2, slabs // (ways * deep), deep, ways), ("mirror",) + SLAB)
    return jax.shard_map(
        on_device,
        mesh=split,
        in_specs=(
            P(SLAB, None, None),
            P("mirror", SLAB, None, None),
            P("mirror", SLAB, None, None),
            P(),
        ),
        out_specs=(
            P("mirror", None, SLAB, None, None),
            P("mirror", None, SLAB, None, None),
            P(SLAB, None, None),
        ),
        check_vma=False,
    )
```

```python
import functools

import jax
import jax.numpy as jnp
import numpy as np
from jax import lax
from jax.experimental import pallas as pl
from jax.experimental.pallas import tpu as pltpu
from jax.sharding import Mesh
from jax.sharding import PartitionSpec as P

SWEEPS = 4
MODULUS_FLOOR = 0.001
EIG_LOWER = 0.05
EIG_UPPER = 1.0
CENTRE = 0.5 * (EIG_UPPER + EIG_LOWER)
HALF_WIDTH = 0.5 * (EIG_UPPER - EIG_LOWER)
DIRECTION = (0.4, -0.3, -1.0)
SLAB = ("y", "z", "x")
ROWS = 8
COLS = 256
OWN = 4
UNROLL = True


def element_matrix():
    poisson = 0.3
    lame_first = poisson / ((1.0 + poisson) * (1.0 - 2.0 * poisson))
    shear_modulus = 0.5 / (1.0 + poisson)
    elastic = np.zeros((6, 6))
    elastic[:3, :3] = lame_first
    for i in range(3):
        elastic[i, i] += 2.0 * shear_modulus
        elastic[i + 3, i + 3] = shear_modulus
    points = [0.5 - 0.5 / np.sqrt(3.0), 0.5 + 0.5 / np.sqrt(3.0)]
    stiffness = np.zeros((24, 24))
    for p in points:
        for q in points:
            for s in points:
                strain = np.zeros((6, 24))
                for corner in range(8):
                    z_bit, y_bit, x_bit = (corner // 4, corner // 2 % 2, corner % 2)
                    weight_z = p if z_bit else 1.0 - p
                    weight_y = q if y_bit else 1.0 - q
                    weight_x = s if x_bit else 1.0 - s
                    slope_z = 1.0 if z_bit else -1.0
                    slope_y = 1.0 if y_bit else -1.0
                    slope_x = 1.0 if x_bit else -1.0
                    grad_x = slope_x * weight_y * weight_z
                    grad_y = weight_x * slope_y * weight_z
                    grad_z = weight_x * weight_y * slope_z
                    c = 3 * corner
                    strain[0, c] = grad_x
                    strain[1, c + 1] = grad_y
                    strain[2, c + 2] = grad_z
                    strain[3, c] = grad_y
                    strain[3, c + 1] = grad_x
                    strain[4, c + 1] = grad_z
                    strain[4, c + 2] = grad_y
                    strain[5, c] = grad_z
                    strain[5, c + 2] = grad_x
                stiffness += strain.T @ elastic @ strain / 8.0
    return stiffness


@functools.lru_cache(None)
def mode_matrix():
    one = np.array([[1.0, 1.0], [-1.0, 1.0]])
    signs = np.kron(np.kron(one, one), one)
    spread = np.kron(signs, np.eye(3)) / 8.0
    matrix = spread @ element_matrix() @ spread.T
    table = {}
    for row in range(24):
        entries = [
            ((col // 3, col % 3), float(matrix[row, col]))
            for col in range(24)
            if abs(matrix[row, col]) > 1e-12
        ]
        if entries:
            table[(row // 3, row % 3)] = entries
    return table


@functools.lru_cache(None)
def row_total():
    totals = np.abs(element_matrix()).sum(axis=1)
    assert np.allclose(totals, totals[0], rtol=1e-12)
    return float(totals[0])


def chebyshev_factors():
    ratio = CENTRE / HALF_WIDTH
    rho = 1.0 / ratio
    factors = []
    for _ in range(1, SWEEPS):
        rho_next = 1.0 / (2.0 * ratio - rho)
        factors.append((rho_next * rho, 2.0 * rho_next / HALF_WIDTH))
        rho = rho_next
    return factors


class Plane:
    def __init__(self, step):
        lane = lax.broadcasted_iota(jnp.int32, (ROWS, COLS), 1)
        row = lax.broadcasted_iota(jnp.int32, (ROWS, COLS), 0)
        self.step = step
        self.lane_not_last = lane < COLS - step
        self.lane_not_first = lane >= step
        self.row_not_last = row < ROWS - step
        self.row_not_first = row >= step

    def next_x(self, v):
        return jnp.where(self.lane_not_last, pltpu.roll(v, COLS - self.step, 1), 0.0)

    def prev_x(self, v):
        return jnp.where(self.lane_not_first, pltpu.roll(v, self.step, 1), 0.0)

    def next_y(self, v):
        return jnp.where(self.row_not_last, pltpu.roll(v, ROWS - self.step, 0), 0.0)

    def prev_y(self, v):
        return jnp.where(self.row_not_first, pltpu.roll(v, self.step, 0), 0.0)

    def corner_sum(self, v):
        v = v + self.prev_x(v)
        return v + self.prev_y(v)

    def forward(self, comps):
        modes = [[None] * 3 for _ in range(4)]
        for c, v in enumerate(comps):
            ahead = self.next_x(v)
            for x_bit, w in enumerate((ahead + v, ahead - v)):
                above = self.next_y(w)
                modes[x_bit][c] = above + w
                modes[2 + x_bit][c] = above - w
        return modes

    def backward(self, modes):
        comps = []
        for c in range(3):
            along = []
            for x_bit in range(2):
                total, change = modes[x_bit][c], modes[2 + x_bit][c]
                along.append((total - change) + self.prev_y(total + change))
            comps.append((along[0] - along[1]) + self.prev_x(along[0] + along[1]))
        return comps

    def element(self, low, high, modulus, scale, with_energy=False):
        modes = {}
        for m in range(4):
            for c in range(3):
                if m > 0:
                    modes[(m, c)] = high[m][c] + low[m][c]
                modes[(4 + m, c)] = high[m][c] - low[m][c]
        forces = {}
        for row, entries in mode_matrix().items():
            total = None
            for col, entry in entries:
                term = modes[col] * np.float32(entry * scale)
                total = term if total is None else total + term
            forces[row] = total
        energy = None
        if with_energy:
            for row, force in forces.items():
                term = modes[row] * force
                energy = term if energy is None else energy + term
        on_low = [[None] * 3 for _ in range(4)]
        on_high = [[None] * 3 for _ in range(4)]
        for m in range(4):
            for c in range(3):
                change = modulus * forces[(4 + m, c)]
                if m > 0:
                    total = modulus * forces[(m, c)]
                    on_low[m][c] = total - change
                    on_high[m][c] = total + change
                else:
                    on_low[m][c] = -change
                    on_high[m][c] = change
        return on_low, on_high, energy


def apply_planes(plane, first, last, load, modulus_at, scale, consume, with_energy=False):
    def flat(modes):
        return tuple(v for mode in modes for v in mode)

    def nested(values):
        return [[values[3 * m + c] for c in range(3)] for m in range(4)]

    def body(p, carry):
        low, pending = nested(carry[:12]), nested(carry[12:])
        high = plane.forward(load(p + 1))
        on_low, on_high, energy = plane.element(low, high, modulus_at(p), scale, with_energy)
        total = [[pending[m][c] + on_low[m][c] for c in range(3)] for m in range(4)]
        consume(p, plane.backward(total), energy)
        return flat(high) + flat(on_high)

    start = flat(plane.forward(load(first - 1)))
    zeros = tuple(jnp.zeros((ROWS, COLS), jnp.float32) for _ in range(12))
    lax.fori_loop(first - 1, last + 1, body, start + zeros, unroll=UNROLL)


class Groups:
    def __init__(self):
        lane = lax.broadcasted_iota(jnp.int32, (ROWS, COLS), 1)
        row = lax.broadcasted_iota(jnp.int32, (ROWS, COLS), 0)
        self.lane_in, self.row_in = lane % 4, row % 4
        self.lane_bits = [lane % 2 == 1, lane // 2 % 2 == 1]
        self.row_bits = [row % 2 == 1, row // 2 % 2 == 1]

    def over_rows(self, v):
        for bit in range(2):
            by = 1 << bit
            v = v + jnp.where(self.row_bits[bit], pltpu.roll(v, by, 0), pltpu.roll(v, ROWS - by, 0))
        return v

    def over_lanes(self, v):
        for bit in range(2):
            by = 1 << bit
            v = v + jnp.where(self.lane_bits[bit], pltpu.roll(v, by, 1), pltpu.roll(v, COLS - by, 1))
        return v

    def both(self, v):
        return self.over_lanes(self.over_rows(v))


def modulus_of(density):
    return MODULUS_FLOOR + density * density * density * (1.0 - MODULUS_FLOOR)


def flip_matrix():
    row = lax.broadcasted_iota(jnp.int32, (128, 128), 0)
    return (row + lax.broadcasted_iota(jnp.int32, (128, 128), 1) == 127).astype(jnp.float32)


def flipped(stacked):
    return jnp.dot(stacked, flip_matrix(), precision=lax.Precision.HIGHEST, preferred_element_type=jnp.float32)


def smooth_kernel(
    slabs, info, own, below, above, edge, smooth, coarse, dens_out, free_out, right_out, mod, x, d, w, right, free, left
):
    plane, groups = Plane(1), Groups()
    slab, sweep_count = info[0], info[2]
    has_below = (slab > 0).astype(jnp.float32)
    has_edge = (slab > 1).astype(jnp.float32)
    has_above = (slab < slabs - 1).astype(jnp.float32)

    halves = [edge[0]] + [source[0, k] for source in (below, own, above) for k in range(OWN)]
    turned = flipped(jnp.concatenate(halves, axis=0))
    insides = [has_edge] + [has_below] * OWN + [None] * OWN + [has_above] * OWN
    for k in range(13):
        density = jnp.concatenate([halves[k], turned[ROWS * k : ROWS * (k + 1)]], axis=1)
        value = modulus_of(density)
        mod[k] = value if insides[k] is None else value * insides[k]
        if 4 <= k < 9:
            dens_out[k - 4] = density

    def both_halves(source, field, k):
        return jnp.concatenate([source[1 + field, k], source[3 + field, k]], axis=1)

    for source, at, inside in ((below, 0, has_below), (own, 4, None), (above, 8, has_above)):
        for k in range(OWN):
            open_node = 1.0 - both_halves(source, 1, k)
            free[at + k] = open_node if inside is None else open_node * inside

    def prepare(q, carry):
        summed = plane.corner_sum(mod[q + 1])
        scaling = np.float32(row_total()) * (carry + summed)
        f = free[q]
        scaling = jnp.where(f > 0.0, scaling, 1.0)
        inverse = 1.0 / scaling
        w[q] = inverse
        return summed

    lax.fori_loop(0, 12, prepare, plane.corner_sum(mod[0]), unroll=UNROLL)
    for source, at in ((below, 0), (own, 4), (above, 8)):
        for k in range(OWN):
            loaded = free[at + k] * both_halves(source, 0, k)
            start = loaded * (w[at + k] * np.float32(1.0 / CENTRE))
            right[at + k] = loaded
            for c in range(3):
                x[c, at + k] = start * np.float32(DIRECTION[c])
                d[c, at + k] = start * np.float32(DIRECTION[c])

    def load(q):
        f = free[q]
        return [f * x[c, q] for c in range(3)]

    def modulus_at(q):
        return mod[q + 1]

    for k, (keep, add) in enumerate(chebyshev_factors(), 1):

        @pl.when(k < sweep_count)
        def _(k=k, keep=keep, add=add):
            def consume(q, forces, _energy):
                f, weight = free[q], w[q] * np.float32(add)
                is_free = f > 0.0
                loaded = right[q]
                for c in range(3):
                    now = x[c, q]
                    image = jnp.where(is_free, forces[c], now)
                    defect = loaded * np.float32(DIRECTION[c]) - image
                    update = np.float32(keep) * d[c, q] + weight * defect
                    d[c, q] = update
                    x[c, q] = now + update

            apply_planes(plane, k, 11 - k, load, modulus_at, 1.0, consume)

    def consume_left(q, forces, _energy):
        is_free = free[q] > 0.0
        for c in range(3):
            image = jnp.where(is_free, forces[c], x[c, q])
            left[c, q - 3] = right[q] * np.float32(DIRECTION[c]) - image

    apply_planes(plane, 4, 7, load, modulus_at, 1.0, consume_left)

    for c in range(3):
        for k in range(6):
            smooth[c, k] = x[c, k + 3]
    fields = [groups.both((left[c, 1] + left[c, 2]) + (left[c, 3] + left[c, 4])) for c in range(3)]
    here = groups.both((mod[5] + mod[6]) + (mod[7] + mod[8])) * np.float32(1.0 / 64.0)
    under = groups.both((mod[1] + mod[2]) + (mod[3] + mod[4])) * np.float32(1.0 / 64.0)
    packed = here
    for c in range(3):
        packed = jnp.where(groups.lane_in == c, fields[c], packed)
    packed = jnp.where(groups.row_in == 0, packed, under)
    coarse[0:2] = packed[0:2]
    coarse[2:4] = packed[4:6]
    for k in range(6):
        free_out[k] = free[k + 3]
    for k in range(OWN):
        right_out[k] = right[k + 4]


def correct_kernel(
    slabs, info, smooth, dens, free, right, gathered, moved, image, slope, sums, window, mod, x, d, w, target, p, fmod, img, energy
):
    coarse_plane, plane, groups = Plane(4), Plane(1), Groups()
    slab, mirror, sweep_count = info[0], info[1], info[3]
    offset = slab % 4
    upper_rows = lax.broadcasted_iota(jnp.int32, (ROWS, COLS), 0) >= 4

    def widened(first, second):
        return jnp.where(upper_rows, jnp.broadcast_to(second, (ROWS, COLS)), jnp.broadcast_to(first, (ROWS, COLS)))

    for k in range(4):
        window[k] = widened(gathered[k, 4:5], gathered[k, 6:7])
        window[4 + k] = widened(gathered[k, 0:1], gathered[k, 2:3])
        window[8 + k] = widened(gathered[4 + k, 4:5], gathered[4 + k, 6:7])

    def unpack(q, carry):
        packed = window[offset + q]
        for c in range(3):
            target[c, q] = groups.over_lanes(jnp.where(groups.lane_in == c, packed, 0.0))
        mod[q + 1] = groups.over_lanes(jnp.where(groups.lane_in == 3, packed, 0.0))
        return carry

    lax.fori_loop(0, 9, unpack, 0, unroll=UNROLL)
    mod[0] = widened(gathered[offset, 5:6], gathered[offset, 7:8])

    def prepare(q, carry):
        summed = coarse_plane.corner_sum(mod[q + 1])
        scaling = np.float32(4.0 * row_total()) * (carry + summed)
        at = slab - 4 + q
        inside = ((at >= 0) & (at < slabs)).astype(jnp.float32)
        inverse = inside / jnp.where(scaling > 0.0, scaling, 1.0)
        w[q] = inverse
        for c in range(3):
            start = target[c, q] * (inverse * np.float32(1.0 / CENTRE))
            x[c, q] = start
            d[c, q] = start
        return summed

    lax.fori_loop(0, 9, prepare, coarse_plane.corner_sum(mod[0]), unroll=UNROLL)

    for k, (keep, add) in enumerate(chebyshev_factors(), 1):

        @pl.when(k < sweep_count)
        def _(k=k, keep=keep, add=add):
            def consume(q, forces, _energy):
                weight = w[q] * np.float32(add)
                for c in range(3):
                    update = np.float32(keep) * d[c, q] + weight * (target[c, q] - forces[c])
                    d[c, q] = update
                    x[c, q] = x[c, q] + update

            apply_planes(
                coarse_plane,
                k,
                8 - k,
                lambda q: [x[c, q] for c in range(3)],
                lambda q: mod[q + 1],
                4.0,
                consume,
            )

    has_below = (slab > 0).astype(jnp.float32)
    for k in range(6):
        for c in range(3):
            p[c, k] = smooth[c, k] + free[k] * x[c, 3 if k == 0 else 5 if k == 5 else 4]
        if k < 5:
            value = modulus_of(dens[k])
            fmod[k] = value * has_below if k == 0 else value

    def consume_image(q, forces, strain):
        is_free = free[q] > 0.0
        for c in range(3):
            img[c, q] = jnp.where(is_free, forces[c], p[c, q])
        energy[q] = strain

    def load_p(q):
        f = free[q]
        return [f * p[c, q] for c in range(3)]

    apply_planes(plane, 1, 4, load_p, lambda q: fmod[q], 1.0, consume_image, True)

    first = jnp.zeros((ROWS, COLS), jnp.float32)
    second = jnp.zeros((ROWS, COLS), jnp.float32)
    half = pl.ds(pl.multiple_of(mirror * 128, 128), 128)
    for k in range(OWN):
        loaded = right[k]
        for c in range(3):
            first = first + (loaded * np.float32(DIRECTION[c])) * p[c, k + 1]
            second = second + p[c, k + 1] * img[c, k + 1]
            moved[c, k] = p[c, k + 1, :, half]
            image[c, k] = img[c, k + 1, :, half]
        density = dens[k + 1]
        energy[k + 1] = np.float32(-3.0 * (1.0 - MODULUS_FLOOR)) * (density * density) * energy[k + 1]
    second_half = jnp.concatenate([energy[k + 1, :, 128:] for k in range(OWN)], axis=0)
    turned = flipped(second_half)
    for k in range(OWN):
        slope[k] = energy[k + 1, :, :128] + turned[ROWS * k : ROWS * (k + 1)]
    lane = lax.broadcasted_iota(jnp.int32, (1, 128), 1)
    dots = jnp.where(lane == 0, jnp.sum(first), jnp.where(lane == 1, jnp.sum(second), 0.0))
    for k in range(sums.shape[0]):
        sums[k] = dots


def scale_kernel(totals, load, fixed, moved, image, slope, displacement, residual, sensitivity):
    total = totals[0]
    for k in range(1, totals.shape[0]):
        total = total + totals[k]
    lane = lax.broadcasted_iota(jnp.int32, (1, 128), 1)
    residual_dot = jnp.sum(jnp.where(lane == 0, total, 0.0), axis=1, keepdims=True)
    curvature = jnp.sum(jnp.where(lane == 1, total, 0.0), axis=1, keepdims=True)
    alpha = jnp.broadcast_to(residual_dot / curvature, (ROWS, 128))
    for k in range(OWN):
        loaded = ((1 - fixed[0, k]) * load[0, k]).astype(jnp.float32)
        for c in range(3):
            displacement[c, k] = alpha * moved[c, k]
            residual[c, k] = loaded * np.float32(DIRECTION[c]) - alpha * image[c, k]
        sensitivity[k] = alpha * (alpha * slope[k])


def call(kernel, outs, ins, scratch=()):
    vmem = pl.BlockSpec(memory_space=pltpu.VMEM)
    smem = pl.BlockSpec(memory_space=pltpu.SMEM)
    return pl.pallas_call(
        kernel,
        out_shape=[jax.ShapeDtypeStruct(shape, jnp.float32) for shape in outs],
        in_specs=[smem if v.ndim == 1 else vmem for v in ins],
        out_specs=[vmem] * len(outs),
        scratch_shapes=[pltpu.VMEM(shape, jnp.float32) for shape in scratch],
        compiler_params=pltpu.CompilerParams(vmem_limit_bytes=16 * 1024 * 1024),
    )(*ins)


def shifted(array, axis, by):
    length = lax.axis_size(axis)
    pairs = [(i, i + by) for i in range(length) if 0 <= i + by < length]
    return lax.ppermute(array, axis, pairs)


def run_smooth(slabs, info, own, below, above, edge):
    plane = (ROWS, COLS)
    field = (3, 12) + plane
    return call(
        functools.partial(smooth_kernel, slabs),
        [(3, 6) + plane, (4, COLS), (5,) + plane, (6,) + plane, (OWN,) + plane],
        [info, own, below, above, edge],
        [(13,) + plane, field, field, (12,) + plane, (12,) + plane, (12,) + plane, (3, 5) + plane],
    )


def run_correct(slabs, group, info, smooth, dens, free, right, gathered):
    plane = (ROWS, COLS)
    coarse_field = (3, 9) + plane
    part = (3, OWN, ROWS, 128)
    return call(
        functools.partial(correct_kernel, slabs),
        [part, part, part[1:], (group, 1, 128)],
        [info, smooth, dens, free, right, gathered],
        [
            (12,) + plane,
            (10,) + plane,
            coarse_field,
            coarse_field,
            (9,) + plane,
            coarse_field,
            (3, 6) + plane,
            (5,) + plane,
            (3, 5) + plane,
            (5,) + plane,
        ],
    )


def on_device(density, load_mask, fixed_mask, sweeps):
    slabs = lax.axis_size(SLAB)
    slab, mirror = lax.axis_index(SLAB), lax.axis_index("mirror")
    info = jnp.concatenate([jnp.stack([slab, mirror]).astype(jnp.int32), sweeps])

    edge = shifted(density[OWN - 1 :], SLAB, 2)
    masks = lax.all_gather(jnp.concatenate([load_mask, fixed_mask], axis=0), "mirror")
    own = jnp.concatenate([density[None], masks.reshape((4,) + density.shape).astype(jnp.float32)], axis=0)
    below = shifted(own, SLAB, 1)
    above = shifted(own, SLAB, -1)

    smooth, coarse, dens, free, right = run_smooth(slabs, info, own, below, above, edge)

    reach = 4
    pairs = [(i, i + reach) for i in range(slabs - reach)]
    pairs += [(slabs + i + reach, slabs + i) for i in range(slabs - reach)]
    arrived = lax.ppermute(coarse, ("mirror",) + SLAB, pairs)
    sent = jnp.broadcast_to(jnp.concatenate([coarse, arrived], axis=0), (8, 8, COLS))
    gathered = lax.all_to_all(sent, ("mirror", "x"), 0, 0)

    part = (3, OWN, ROWS, 128)
    group = lax.axis_size(("y", "x"))
    moved, image, slope, sums = run_correct(slabs, group, info, smooth, dens, free, right, gathered)
    sums = lax.all_to_all(sums, ("y", "x"), 0, 0)
    length = lax.axis_size("z")
    sums = jnp.broadcast_to(jnp.sum(sums, axis=0), (length, 1, 128))
    sums = lax.all_to_all(sums, "z", 0, 0)
    displacement, residual, sensitivity = call(
        scale_kernel, [part, part, part[1:]], [sums, load_mask, fixed_mask, moved, image, slope]
    )
    return displacement[None], residual[None], sensitivity


def solution(mesh):
    slabs = mesh.shape["slab"]
    ways = 4
    deep = min(16, slabs // ways)
    split = Mesh(mesh.devices.reshape(2, slabs // (ways * deep), deep, ways), ("mirror",) + SLAB)
    return jax.shard_map(
        on_device,
        mesh=split,
        in_specs=(
            P(SLAB, None, None),
            P("mirror", SLAB, None, None),
            P("mirror", SLAB, None, None),
            P(),
        ),
        out_specs=(
            P("mirror", None, SLAB, None, None),
            P("mirror", None, SLAB, None, None),
            P(SLAB, None, None),
        ),
        check_vma=False,
    )
```

```python
import functools

import jax
import jax.numpy as jnp
import numpy as np
from jax import lax
from jax.experimental import pallas as pl
from jax.experimental.pallas import tpu as pltpu
from jax.sharding import Mesh
from jax.sharding import PartitionSpec as P

SWEEPS = 4
MODULUS_FLOOR = 0.001
EIG_LOWER = 0.05
EIG_UPPER = 1.0
CENTRE = 0.5 * (EIG_UPPER + EIG_LOWER)
HALF_WIDTH = 0.5 * (EIG_UPPER - EIG_LOWER)
DIRECTION = (0.4, -0.3, -1.0)
SLAB = ("y", "z", "x")
ROWS = 8
COLS = 256
OWN = 4
DENSITY, LOAD, FIXED, FIELDS = 0, 1, 2, 3


def element_matrix():
    poisson = 0.3
    lame_first = poisson / ((1.0 + poisson) * (1.0 - 2.0 * poisson))
    shear_modulus = 0.5 / (1.0 + poisson)
    elastic = np.zeros((6, 6))
    elastic[:3, :3] = lame_first
    for i in range(3):
        elastic[i, i] += 2.0 * shear_modulus
        elastic[i + 3, i + 3] = shear_modulus
    points = [0.5 - 0.5 / np.sqrt(3.0), 0.5 + 0.5 / np.sqrt(3.0)]
    stiffness = np.zeros((24, 24))
    for p in points:
        for q in points:
            for s in points:
                strain = np.zeros((6, 24))
                for corner in range(8):
                    z_bit, y_bit, x_bit = (corner // 4, corner // 2 % 2, corner % 2)
                    weight_z = p if z_bit else 1.0 - p
                    weight_y = q if y_bit else 1.0 - q
                    weight_x = s if x_bit else 1.0 - s
                    slope_z = 1.0 if z_bit else -1.0
                    slope_y = 1.0 if y_bit else -1.0
                    slope_x = 1.0 if x_bit else -1.0
                    grad_x = slope_x * weight_y * weight_z
                    grad_y = weight_x * slope_y * weight_z
                    grad_z = weight_x * weight_y * slope_z
                    c = 3 * corner
                    strain[0, c] = grad_x
                    strain[1, c + 1] = grad_y
                    strain[2, c + 2] = grad_z
                    strain[3, c] = grad_y
                    strain[3, c + 1] = grad_x
                    strain[4, c + 1] = grad_z
                    strain[4, c + 2] = grad_y
                    strain[5, c] = grad_z
                    strain[5, c + 2] = grad_x
                stiffness += strain.T @ elastic @ strain / 8.0
    return stiffness


@functools.lru_cache(None)
def mode_matrix():
    one = np.array([[1.0, 1.0], [-1.0, 1.0]])
    signs = np.kron(np.kron(one, one), one)
    spread = np.kron(signs, np.eye(3)) / 8.0
    matrix = spread @ element_matrix() @ spread.T
    table = {}
    for row in range(24):
        entries = [
            ((col // 3, col % 3), float(matrix[row, col]))
            for col in range(24)
            if abs(matrix[row, col]) > 1e-12
        ]
        if entries:
            table[(row // 3, row % 3)] = entries
    return table


@functools.lru_cache(None)
def row_total():
    totals = np.abs(element_matrix()).sum(axis=1)
    assert np.allclose(totals, totals[0], rtol=1e-12)
    return float(totals[0])


def chebyshev_factors():
    ratio = CENTRE / HALF_WIDTH
    rho = 1.0 / ratio
    factors = []
    for _ in range(1, SWEEPS):
        rho_next = 1.0 / (2.0 * ratio - rho)
        factors.append((rho_next * rho, 2.0 * rho_next / HALF_WIDTH))
        rho = rho_next
    return factors


class Plane:
    def __init__(self, step):
        lane = lax.broadcasted_iota(jnp.int32, (ROWS, COLS), 1)
        row = lax.broadcasted_iota(jnp.int32, (ROWS, COLS), 0)
        self.step = step
        self.lane_not_last = lane < COLS - step
        self.lane_not_first = lane >= step
        self.row_not_last = row < ROWS - step
        self.row_not_first = row >= step

    def next_x(self, v):
        return jnp.where(self.lane_not_last, pltpu.roll(v, COLS - self.step, 1), 0.0)

    def prev_x(self, v):
        return jnp.where(self.lane_not_first, pltpu.roll(v, self.step, 1), 0.0)

    def next_y(self, v):
        return jnp.where(self.row_not_last, pltpu.roll(v, ROWS - self.step, 0), 0.0)

    def prev_y(self, v):
        return jnp.where(self.row_not_first, pltpu.roll(v, self.step, 0), 0.0)

    def corner_sum(self, v):
        v = v + self.prev_x(v)
        return v + self.prev_y(v)

    def forward(self, comps):
        modes = [[None] * 3 for _ in range(4)]
        for c, v in enumerate(comps):
            ahead = self.next_x(v)
            for x_bit, w in enumerate((ahead + v, ahead - v)):
                above = self.next_y(w)
                modes[x_bit][c] = above + w
                modes[2 + x_bit][c] = above - w
        return modes

    def backward(self, modes):
        comps = []
        for c in range(3):
            along = []
            for x_bit in range(2):
                total, change = modes[x_bit][c], modes[2 + x_bit][c]
                along.append((total - change) + self.prev_y(total + change))
            comps.append((along[0] - along[1]) + self.prev_x(along[0] + along[1]))
        return comps

    def element(self, low, high, modulus, scale, with_energy=False):
        modes = {}
        for m in range(4):
            for c in range(3):
                if m > 0:
                    modes[(m, c)] = high[m][c] + low[m][c]
                modes[(4 + m, c)] = high[m][c] - low[m][c]
        forces = {}
        for row, entries in mode_matrix().items():
            total = None
            for col, entry in entries:
                term = modes[col] * np.float32(entry * scale)
                total = term if total is None else total + term
            forces[row] = total
        energy = None
        if with_energy:
            for row, force in forces.items():
                term = modes[row] * force
                energy = term if energy is None else energy + term
        on_low = [[None] * 3 for _ in range(4)]
        on_high = [[None] * 3 for _ in range(4)]
        for m in range(4):
            for c in range(3):
                change = modulus * forces[(4 + m, c)]
                if m > 0:
                    total = modulus * forces[(m, c)]
                    on_low[m][c] = total - change
                    on_high[m][c] = total + change
                else:
                    on_low[m][c] = -change
                    on_high[m][c] = change
        return on_low, on_high, energy


def apply_planes(plane, first, last, load, modulus_at, scale, consume, with_energy=False):
    def flat(modes):
        return tuple(v for mode in modes for v in mode)

    def nested(values):
        return [[values[3 * m + c] for c in range(3)] for m in range(4)]

    def body(q, carry):
        low, pending = nested(carry[:12]), nested(carry[12:])
        high = plane.forward(load(q + 1))
        on_low, on_high, energy = plane.element(low, high, modulus_at(q), scale, with_energy)
        total = [[pending[m][c] + on_low[m][c] for c in range(3)] for m in range(4)]
        consume(q, plane.backward(total), energy)
        return flat(high) + flat(on_high)

    start = flat(plane.forward(load(first)))
    zeros = tuple(jnp.zeros((ROWS, COLS), jnp.float32) for _ in range(12))
    carry = lax.fori_loop(first, last + 1, body, start + zeros, unroll=True)
    return lambda: plane.backward(nested(carry[12:]))


class Groups:
    def __init__(self):
        lane = lax.broadcasted_iota(jnp.int32, (ROWS, COLS), 1)
        row = lax.broadcasted_iota(jnp.int32, (ROWS, COLS), 0)
        self.lane_in, self.row_in = lane % 4, row % 4
        self.lane_bits = [lane % 2 == 1, lane // 2 % 2 == 1]
        self.row_bits = [row % 2 == 1, row // 2 % 2 == 1]

    def over_rows(self, v):
        for bit in range(2):
            by = 1 << bit
            v = v + jnp.where(self.row_bits[bit], pltpu.roll(v, by, 0), pltpu.roll(v, ROWS - by, 0))
        return v

    def over_lanes(self, v):
        for bit in range(2):
            by = 1 << bit
            v = v + jnp.where(self.lane_bits[bit], pltpu.roll(v, by, 1), pltpu.roll(v, COLS - by, 1))
        return v

    def both(self, v):
        return self.over_lanes(self.over_rows(v))


def modulus_of(density):
    return MODULUS_FLOOR + density * density * density * (1.0 - MODULUS_FLOOR)


def flip_matrix():
    row = lax.broadcasted_iota(jnp.int32, (128, 128), 0)
    return (row + lax.broadcasted_iota(jnp.int32, (128, 128), 1) == 127).astype(jnp.float32)


def flipped(stacked):
    return jnp.dot(stacked, flip_matrix(), precision=lax.Precision.HIGHEST, preferred_element_type=jnp.float32)


def both_halves(source, field, k):
    return jnp.concatenate([source[field, k], source[FIELDS + field, k]], axis=1)


def smooth_kernel(
    slabs, info, own, below, above, smooth, coarse, dens_out, free_out, right_out, mod, x, d, w, right, free, left
):
    plane, groups = Plane(1), Groups()
    slab, sweep_count = info[0], info[2]
    has_below = (slab > 0).astype(jnp.float32)
    has_above = (slab < slabs - 1).astype(jnp.float32)

    places = [(below, k, has_below) for k in range(OWN)]
    places += [(own, k, None) for k in range(OWN)]
    places += [(above, k, has_above) for k in range(OWN)]
    turned = flipped(jnp.concatenate([source[DENSITY, k] for source, k, _ in places], axis=0))
    for e, (source, k, inside) in enumerate(places):
        density = jnp.concatenate([source[DENSITY, k], turned[ROWS * e : ROWS * (e + 1)]], axis=1)
        value = modulus_of(density)
        mod[e] = value if inside is None else value * inside
        if source is own:
            dens_out[k] = density
        if e > 0:
            open_node = 1.0 - both_halves(source, FIXED, k)
            free[e - 1] = open_node if inside is None else open_node * inside

    summed = plane.corner_sum(mod[0])
    for q, (source, k, _) in enumerate(places[1:]):
        lower, summed = summed, plane.corner_sum(mod[q + 1])
        scaling = np.float32(row_total()) * (lower + summed)
        inverse = 1.0 / jnp.where(free[q] > 0.0, scaling, 1.0)
        w[q] = inverse
        loaded = free[q] * both_halves(source, LOAD, k)
        right[q] = loaded
        start = loaded * (inverse * np.float32(1.0 / CENTRE))
        for c in range(3):
            x[c, q] = start * np.float32(DIRECTION[c])
            d[c, q] = start * np.float32(DIRECTION[c])

    def load(q):
        f = free[q]
        return [f * x[c, q] for c in range(3)]

    def modulus_at(q):
        return mod[q + 1]

    for k, (keep, add) in enumerate(chebyshev_factors(), 1):

        @pl.when(k < sweep_count)
        def _(k=k, keep=keep, add=add):
            def consume(q, forces, _energy):
                f, weight = free[q], w[q] * np.float32(add)
                is_free = f > 0.0
                loaded = right[q]
                for c in range(3):
                    now = x[c, q]
                    image = jnp.where(is_free, forces[c], now)
                    defect = loaded * np.float32(DIRECTION[c]) - image
                    update = np.float32(keep) * d[c, q] + weight * defect
                    d[c, q] = update
                    x[c, q] = now + update

            apply_planes(plane, k - 1, 10 - k, load, modulus_at, 1.0, consume)

    def consume_left(q, forces, _energy):
        is_free = free[q] > 0.0
        for c in range(3):
            image = jnp.where(is_free, forces[c], x[c, q])
            left[c, q - 3] = right[q] * np.float32(DIRECTION[c]) - image

    rest = apply_planes(plane, 3, 6, load, modulus_at, 1.0, consume_left)()

    odd = groups.lane_bits[0]
    packed = groups.both((mod[4] + mod[5]) + (mod[6] + mod[7])) * np.float32(1.0 / 64.0)
    for c in range(3):
        for k in range(5):
            smooth[c, k] = x[c, k + 3]
        mine = groups.both((left[c, 0] + left[c, 1]) + (left[c, 2] + left[c, 3]))
        passed = groups.both(free[7] * -rest[c])
        packed = jnp.where(groups.row_in == c, jnp.where(odd, passed, mine), packed)
    coarse[...] = packed
    for k in range(5):
        free_out[k] = free[k + 3]
    for k in range(OWN):
        right_out[k] = right[k + 3]


def correct_kernel(
    slabs, info, smooth, dens, free, right, gathered, moved, image, passed, slope, sums, mod, x, d, w, target, p, own_mod, energy
):
    coarse_plane, plane, groups = Plane(4), Plane(1), Groups()
    slab, mirror, sweep_count = info[0], info[1], info[3]
    offset = slab % 4
    upper_rows = lax.broadcasted_iota(jnp.int32, (ROWS, COLS), 0) >= 4
    odd = groups.lane_bits[0]
    groups_of = [(k, ROWS) for k in range(4)] + [(k, 0) for k in range(4)] + [(4 + k, ROWS) for k in range(4)]

    def unpack(field, j):
        block, row = groups_of[j]
        first = gathered[block, row + field : row + field + 1]
        second = gathered[block, row + 4 + field : row + 5 + field]
        return jnp.where(upper_rows, jnp.broadcast_to(second, (ROWS, COLS)), jnp.broadcast_to(first, (ROWS, COLS)))

    for lead in range(4):

        @pl.when(offset == lead)
        def _(lead=lead):
            for q in range(9):
                mod[q] = unpack(3, lead + q)
            for c in range(3):
                lower = None
                for q in range(9):
                    value = unpack(c, lead + q)
                    if q > 0:
                        part = jnp.where(odd, pltpu.roll(value, 1, 1), value)
                        target[c, q - 1] = part + jnp.where(odd, lower, pltpu.roll(lower, COLS - 1, 1))
                    lower = value

    summed = coarse_plane.corner_sum(mod[0])
    for q in range(8):
        lower, summed = summed, coarse_plane.corner_sum(mod[q + 1])
        scaling = np.float32(4.0 * row_total()) * (lower + summed)
        at = slab - 3 + q
        inside = ((at >= 0) & (at < slabs)).astype(jnp.float32)
        inverse = inside / jnp.where(scaling > 0.0, scaling, 1.0)
        w[q] = inverse
        for c in range(3):
            start = target[c, q] * (inverse * np.float32(1.0 / CENTRE))
            x[c, q] = start
            d[c, q] = start

    for k, (keep, add) in enumerate(chebyshev_factors(), 1):

        @pl.when(k < sweep_count)
        def _(k=k, keep=keep, add=add):
            def consume(q, forces, _energy):
                weight = w[q] * np.float32(add)
                for c in range(3):
                    update = np.float32(keep) * d[c, q] + weight * (target[c, q] - forces[c])
                    d[c, q] = update
                    x[c, q] = x[c, q] + update

            apply_planes(
                coarse_plane,
                k - 1,
                7 - k,
                lambda q: [x[c, q] for c in range(3)],
                lambda q: mod[q + 1],
                4.0,
                consume,
            )

    half = pl.ds(pl.multiple_of(mirror * 128, 128), 128)
    for k in range(5):
        for c in range(3):
            p[c, k] = smooth[c, k] + free[k] * x[c, 4 if k == 4 else 3]
    for k in range(OWN):
        own_mod[k] = modulus_of(dens[k])

    def consume_image(q, forces, strain):
        for c in range(3):
            x[c, q] = forces[c]
        energy[q] = strain

    def load_p(q):
        f = free[q]
        return [f * p[c, q] for c in range(3)]

    rest = apply_planes(plane, 0, 3, load_p, lambda q: own_mod[q], 1.0, consume_image, True)()

    first = jnp.zeros((ROWS, COLS), jnp.float32)
    second = jnp.zeros((ROWS, COLS), jnp.float32)
    for c in range(3):
        x[c, 4] = rest[c]
        passed[c] = x[c, 4, :, half]
    for k in range(OWN):
        second = second + own_mod[k] * energy[k]
        for c in range(3):
            value = p[c, k]
            first = first + (right[k] * np.float32(DIRECTION[c])) * value
            second = second + (1.0 - free[k]) * (value * value)
            moved[c, k] = p[c, k, :, half]
            image[c, k] = x[c, k, :, half]
        density = dens[k]
        energy[k] = np.float32(-3.0 * (1.0 - MODULUS_FLOOR)) * (density * density) * energy[k]
    turned = flipped(jnp.concatenate([energy[k, :, 128:] for k in range(OWN)], axis=0))
    for k in range(OWN):
        slope[k] = energy[k, :, :128] + turned[ROWS * k : ROWS * (k + 1)]
    lane = lax.broadcasted_iota(jnp.int32, (1, 128), 1)
    dots = jnp.where(lane == 0, jnp.sum(first), jnp.where(lane == 1, jnp.sum(second), 0.0))
    for k in range(sums.shape[0]):
        sums[k] = dots


def scale_kernel(totals, load, fixed, moved, image, arrived, slope, displacement, residual, sensitivity):
    total = totals[0]
    for k in range(1, totals.shape[0]):
        total = total + totals[k]
    lane = lax.broadcasted_iota(jnp.int32, (1, 128), 1)
    residual_dot = jnp.sum(jnp.where(lane == 0, total, 0.0), axis=1, keepdims=True)
    curvature = jnp.sum(jnp.where(lane == 1, total, 0.0), axis=1, keepdims=True)
    alpha = jnp.broadcast_to(residual_dot / curvature, (ROWS, 128))
    for k in range(OWN):
        loaded = ((1 - fixed[0, k]) * load[0, k]).astype(jnp.float32)
        for c in range(3):
            displacement[c, k] = alpha * moved[c, k]
            forces = image[c, k] + arrived[c] if k == 0 else image[c, k]
            forces = jnp.where(fixed[0, k] == 0, forces, moved[c, k])
            residual[c, k] = loaded * np.float32(DIRECTION[c]) - alpha * forces
        sensitivity[k] = alpha * (alpha * slope[k])


def call(kernel, outs, ins, scratch=()):
    vmem = pl.BlockSpec(memory_space=pltpu.VMEM)
    smem = pl.BlockSpec(memory_space=pltpu.SMEM)
    return pl.pallas_call(
        kernel,
        out_shape=[jax.ShapeDtypeStruct(shape, jnp.float32) for shape in outs],
        in_specs=[smem if v.ndim == 1 else vmem for v in ins],
        out_specs=[vmem] * len(outs),
        scratch_shapes=[pltpu.VMEM(shape, jnp.float32) for shape in scratch],
        compiler_params=pltpu.CompilerParams(vmem_limit_bytes=16 * 1024 * 1024),
    )(*ins)


def shifted(array, axis, by):
    length = lax.axis_size(axis)
    pairs = [(i, i + by) for i in range(length) if 0 <= i + by < length]
    return lax.ppermute(array, axis, pairs)


def run_smooth(slabs, info, own, below, above):
    plane = (ROWS, COLS)
    field = (3, 11) + plane
    return call(
        functools.partial(smooth_kernel, slabs),
        [(3, 5) + plane, plane, (OWN,) + plane, (5,) + plane, (OWN,) + plane],
        [info, own, below, above],
        [(12,) + plane, field, field, (11,) + plane, (11,) + plane, (11,) + plane, (3, 4) + plane],
    )


def run_correct(slabs, group, info, smooth, dens, free, right, gathered):
    plane = (ROWS, COLS)
    field = (3, 8) + plane
    part = (3, OWN, ROWS, 128)
    return call(
        functools.partial(correct_kernel, slabs),
        [part, part, (3, ROWS, 128), part[1:], (group, 1, 128)],
        [info, smooth, dens, free, right, gathered],
        [(9,) + plane, field, field, (8,) + plane, field, (3, 5) + plane, (OWN,) + plane, (OWN,) + plane],
    )


def on_device(density, load_mask, fixed_mask, sweeps):
    slabs = lax.axis_size(SLAB)
    slab, mirror = lax.axis_index(SLAB), lax.axis_index("mirror")
    info = jnp.concatenate([jnp.stack([slab, mirror]).astype(jnp.int32), sweeps])

    here = jnp.concatenate([density[None], load_mask.astype(jnp.float32), fixed_mask.astype(jnp.float32)], axis=0)
    own = lax.all_gather(here, "mirror").reshape((2 * FIELDS,) + density.shape)
    below = shifted(own, SLAB, 1)
    above = shifted(own, SLAB, -1)
    smooth, coarse, dens, free, right = run_smooth(slabs, info, own, below, above)

    reach = 4
    pairs = [(i, i + reach) for i in range(slabs - reach)]
    pairs += [(slabs + i + reach, slabs + i) for i in range(slabs - reach)]
    arrived = lax.ppermute(coarse, ("mirror",) + SLAB, pairs)
    sent = jnp.broadcast_to(jnp.concatenate([coarse, arrived], axis=0), (8, 2 * ROWS, COLS))
    gathered = lax.all_to_all(sent, ("mirror", "x"), 0, 0)

    part = (3, OWN, ROWS, 128)
    group = lax.axis_size(("y", "x"))
    moved, image, passed, slope, sums = run_correct(slabs, group, info, smooth, dens, free, right, gathered)
    added = shifted(passed, SLAB, 1)
    sums = lax.all_to_all(sums, ("y", "x"), 0, 0)
    length = lax.axis_size("z")
    sums = jnp.broadcast_to(jnp.sum(sums, axis=0), (length, 1, 128))
    sums = lax.all_to_all(sums, "z", 0, 0)
    displacement, residual, sensitivity = call(
        scale_kernel, [part, part, part[1:]], [sums, load_mask, fixed_mask, moved, image, added, slope]
    )
    return displacement[None], residual[None], sensitivity


def solution(mesh):
    slabs = mesh.shape["slab"]
    ways = 4
    deep = min(16, slabs // ways)
    split = Mesh(mesh.devices.reshape(2, slabs // (ways * deep), deep, ways), ("mirror",) + SLAB)
    return jax.shard_map(
        on_device,
        mesh=split,
        in_specs=(
            P(SLAB, None, None),
            P("mirror", SLAB, None, None),
            P("mirror", SLAB, None, None),
            P(),
        ),
        out_specs=(
            P("mirror", None, SLAB, None, None),
            P("mirror", None, SLAB, None, None),
            P(SLAB, None, None),
        ),
        check_vma=False,
    )
```

```python
import functools

import jax
import jax.numpy as jnp
import numpy as np
from jax import lax
from jax.experimental import pallas as pl
from jax.experimental.pallas import tpu as pltpu
from jax.sharding import Mesh
from jax.sharding import PartitionSpec as P

SWEEPS = 4
MODULUS_FLOOR = 0.001
EIG_LOWER = 0.05
EIG_UPPER = 1.0
CENTRE = 0.5 * (EIG_UPPER + EIG_LOWER)
HALF_WIDTH = 0.5 * (EIG_UPPER - EIG_LOWER)
DIRECTION = (0.4, -0.3, -1.0)
SLAB = ("y", "z", "x")
ROWS = 8
COLS = 256
OWN = 4
LOAD, FIXED = 0, 1


def element_matrix():
    poisson = 0.3
    lame_first = poisson / ((1.0 + poisson) * (1.0 - 2.0 * poisson))
    shear_modulus = 0.5 / (1.0 + poisson)
    elastic = np.zeros((6, 6))
    elastic[:3, :3] = lame_first
    for i in range(3):
        elastic[i, i] += 2.0 * shear_modulus
        elastic[i + 3, i + 3] = shear_modulus
    points = [0.5 - 0.5 / np.sqrt(3.0), 0.5 + 0.5 / np.sqrt(3.0)]
    stiffness = np.zeros((24, 24))
    for p in points:
        for q in points:
            for s in points:
                strain = np.zeros((6, 24))
                for corner in range(8):
                    z_bit, y_bit, x_bit = (corner // 4, corner // 2 % 2, corner % 2)
                    weight_z = p if z_bit else 1.0 - p
                    weight_y = q if y_bit else 1.0 - q
                    weight_x = s if x_bit else 1.0 - s
                    slope_z = 1.0 if z_bit else -1.0
                    slope_y = 1.0 if y_bit else -1.0
                    slope_x = 1.0 if x_bit else -1.0
                    grad_x = slope_x * weight_y * weight_z
                    grad_y = weight_x * slope_y * weight_z
                    grad_z = weight_x * weight_y * slope_z
                    c = 3 * corner
                    strain[0, c] = grad_x
                    strain[1, c + 1] = grad_y
                    strain[2, c + 2] = grad_z
                    strain[3, c] = grad_y
                    strain[3, c + 1] = grad_x
                    strain[4, c + 1] = grad_z
                    strain[4, c + 2] = grad_y
                    strain[5, c] = grad_z
                    strain[5, c + 2] = grad_x
                stiffness += strain.T @ elastic @ strain / 8.0
    return stiffness


@functools.lru_cache(None)
def mode_matrix():
    one = np.array([[1.0, 1.0], [-1.0, 1.0]])
    signs = np.kron(np.kron(one, one), one)
    spread = np.kron(signs, np.eye(3)) / 8.0
    matrix = spread @ element_matrix() @ spread.T
    table = {}
    for row in range(24):
        entries = [
            ((col // 3, col % 3), float(matrix[row, col]))
            for col in range(24)
            if abs(matrix[row, col]) > 1e-12
        ]
        if entries:
            table[(row // 3, row % 3)] = entries
    return table


@functools.lru_cache(None)
def row_total():
    totals = np.abs(element_matrix()).sum(axis=1)
    assert np.allclose(totals, totals[0], rtol=1e-12)
    return float(totals[0])


def chebyshev_factors():
    ratio = CENTRE / HALF_WIDTH
    rho = 1.0 / ratio
    factors = []
    for _ in range(1, SWEEPS):
        rho_next = 1.0 / (2.0 * ratio - rho)
        factors.append((rho_next * rho, 2.0 * rho_next / HALF_WIDTH))
        rho = rho_next
    return factors


class Plane:
    def __init__(self, step):
        lane = lax.broadcasted_iota(jnp.int32, (ROWS, COLS), 1)
        row = lax.broadcasted_iota(jnp.int32, (ROWS, COLS), 0)
        self.step = step
        self.lane_not_last = lane < COLS - step
        self.lane_not_first = lane >= step
        self.row_not_last = row < ROWS - step
        self.row_not_first = row >= step

    def next_x(self, v):
        return jnp.where(self.lane_not_last, pltpu.roll(v, COLS - self.step, 1), 0.0)

    def prev_x(self, v):
        return jnp.where(self.lane_not_first, pltpu.roll(v, self.step, 1), 0.0)

    def next_y(self, v):
        return jnp.where(self.row_not_last, pltpu.roll(v, ROWS - self.step, 0), 0.0)

    def prev_y(self, v):
        return jnp.where(self.row_not_first, pltpu.roll(v, self.step, 0), 0.0)

    def corner_sum(self, v):
        v = v + self.prev_x(v)
        return v + self.prev_y(v)

    def forward(self, comps):
        modes = [[None] * 3 for _ in range(4)]
        for c, v in enumerate(comps):
            ahead = self.next_x(v)
            for x_bit, w in enumerate((ahead + v, ahead - v)):
                above = self.next_y(w)
                modes[x_bit][c] = above + w
                modes[2 + x_bit][c] = above - w
        return modes

    def backward(self, modes):
        comps = []
        for c in range(3):
            along = []
            for x_bit in range(2):
                total, change = modes[x_bit][c], modes[2 + x_bit][c]
                along.append((total - change) + self.prev_y(total + change))
            comps.append((along[0] - along[1]) + self.prev_x(along[0] + along[1]))
        return comps

    def element(self, low, high, modulus, scale, with_energy=False):
        modes = {}
        for m in range(4):
            for c in range(3):
                if m > 0:
                    modes[(m, c)] = high[m][c] + low[m][c]
                modes[(4 + m, c)] = high[m][c] - low[m][c]
        forces = {}
        for row, entries in mode_matrix().items():
            total = None
            for col, entry in entries:
                term = modes[col] * np.float32(entry * scale)
                total = term if total is None else total + term
            forces[row] = total
        energy = None
        if with_energy:
            for row, force in forces.items():
                term = modes[row] * force
                energy = term if energy is None else energy + term
        on_low = [[None] * 3 for _ in range(4)]
        on_high = [[None] * 3 for _ in range(4)]
        for m in range(4):
            for c in range(3):
                change = modulus * forces[(4 + m, c)]
                if m > 0:
                    total = modulus * forces[(m, c)]
                    on_low[m][c] = total - change
                    on_high[m][c] = total + change
                else:
                    on_low[m][c] = -change
                    on_high[m][c] = change
        return on_low, on_high, energy


def apply_planes(plane, first, last, load, modulus_at, scale, consume, with_energy=False):
    def flat(modes):
        return tuple(v for mode in modes for v in mode)

    def nested(values):
        return [[values[3 * m + c] for c in range(3)] for m in range(4)]

    def body(q, carry):
        low, pending = nested(carry[:12]), nested(carry[12:])
        high = plane.forward(load(q + 1))
        on_low, on_high, energy = plane.element(low, high, modulus_at(q), scale, with_energy)
        total = [[pending[m][c] + on_low[m][c] for c in range(3)] for m in range(4)]
        consume(q, plane.backward(total), energy)
        return flat(high) + flat(on_high)

    start = flat(plane.forward(load(first)))
    zeros = tuple(jnp.zeros((ROWS, COLS), jnp.float32) for _ in range(12))
    carry = lax.fori_loop(first, last + 1, body, start + zeros, unroll=True)
    return lambda: plane.backward(nested(carry[12:]))


class Groups:
    def __init__(self):
        lane = lax.broadcasted_iota(jnp.int32, (ROWS, COLS), 1)
        row = lax.broadcasted_iota(jnp.int32, (ROWS, COLS), 0)
        self.lane_in, self.row_in = lane % 4, row % 4
        self.lane_bits = [lane % 2 == 1, lane // 2 % 2 == 1]
        self.row_bits = [row % 2 == 1, row // 2 % 2 == 1]

    def over_rows(self, v):
        for bit in range(2):
            by = 1 << bit
            v = v + jnp.where(self.row_bits[bit], pltpu.roll(v, by, 0), pltpu.roll(v, ROWS - by, 0))
        return v

    def over_lanes(self, v):
        for bit in range(2):
            by = 1 << bit
            v = v + jnp.where(self.lane_bits[bit], pltpu.roll(v, by, 1), pltpu.roll(v, COLS - by, 1))
        return v

    def both(self, v):
        return self.over_lanes(self.over_rows(v))


def modulus_of(density):
    return MODULUS_FLOOR + density * density * density * (1.0 - MODULUS_FLOOR)


def flip_matrix():
    row = lax.broadcasted_iota(jnp.int32, (128, 128), 0)
    return (row + lax.broadcasted_iota(jnp.int32, (128, 128), 1) == 127).astype(jnp.float32)


def flipped(stacked):
    return jnp.dot(stacked, flip_matrix(), precision=lax.Precision.HIGHEST, preferred_element_type=jnp.float32)


def pack_kernel(density, load, fixed, packed):
    packed[0] = density[...]
    packed[1 + LOAD] = load[0].astype(jnp.float32)
    packed[1 + FIXED] = fixed[0].astype(jnp.float32)


def smooth_kernel(
    slabs, info, own, below, above, masks, smooth, coarse, dens_out, free_out, right_out, mod, x, d, w, right, free, left
):
    plane, groups = Plane(1), Groups()
    slab, sweep_count = info[0], info[2]
    has_below = (slab > 0).astype(jnp.float32)
    has_above = (slab < slabs - 1).astype(jnp.float32)

    def both_halves(source, field, k):
        at = 2 * (0 if source is below else 1 if source is own else 2) + field
        return jnp.concatenate([masks[at, k], masks[6 + at, k]], axis=1)

    places = [(below, k, has_below) for k in range(OWN)]
    places += [(own, k, None) for k in range(OWN)]
    places += [(above, k, has_above) for k in range(OWN)]
    turned = flipped(jnp.concatenate([source[0, k] for source, k, _ in places], axis=0))
    for e, (source, k, inside) in enumerate(places):
        density = jnp.concatenate([source[0, k], turned[ROWS * e : ROWS * (e + 1)]], axis=1)
        value = modulus_of(density)
        mod[e] = value if inside is None else value * inside
        if source is own:
            dens_out[k] = density
        if e > 0:
            open_node = 1.0 - both_halves(source, FIXED, k)
            free[e - 1] = open_node if inside is None else open_node * inside

    summed = plane.corner_sum(mod[0])
    for q, (source, k, _) in enumerate(places[1:]):
        lower, summed = summed, plane.corner_sum(mod[q + 1])
        scaling = np.float32(row_total()) * (lower + summed)
        inverse = 1.0 / jnp.where(free[q] > 0.0, scaling, 1.0)
        w[q] = inverse
        loaded = free[q] * both_halves(source, LOAD, k)
        right[q] = loaded
        start = loaded * (inverse * np.float32(1.0 / CENTRE))
        for c in range(3):
            x[c, q] = start * np.float32(DIRECTION[c])
            d[c, q] = start * np.float32(DIRECTION[c])

    def load(q):
        f = free[q]
        return [f * x[c, q] for c in range(3)]

    def modulus_at(q):
        return mod[q + 1]

    for k, (keep, add) in enumerate(chebyshev_factors(), 1):

        @pl.when(k < sweep_count)
        def _(k=k, keep=keep, add=add):
            def consume(q, forces, _energy):
                f, weight = free[q], w[q] * np.float32(add)
                is_free = f > 0.0
                loaded = right[q]
                for c in range(3):
                    now = x[c, q]
                    image = jnp.where(is_free, forces[c], now)
                    defect = loaded * np.float32(DIRECTION[c]) - image
                    update = np.float32(keep) * d[c, q] + weight * defect
                    d[c, q] = update
                    x[c, q] = now + update

            apply_planes(plane, k - 1, 10 - k, load, modulus_at, 1.0, consume)

    def consume_left(q, forces, _energy):
        is_free = free[q] > 0.0
        for c in range(3):
            image = jnp.where(is_free, forces[c], x[c, q])
            left[c, q - 3] = right[q] * np.float32(DIRECTION[c]) - image

    rest = apply_planes(plane, 3, 6, load, modulus_at, 1.0, consume_left)()

    odd = groups.lane_bits[0]
    packed = groups.both((mod[4] + mod[5]) + (mod[6] + mod[7])) * np.float32(1.0 / 64.0)
    for c in range(3):
        for k in range(5):
            smooth[c, k] = x[c, k + 3]
        mine = groups.both((left[c, 0] + left[c, 1]) + (left[c, 2] + left[c, 3]))
        passed = groups.both(free[7] * -rest[c])
        packed = jnp.where(groups.row_in == c, jnp.where(odd, passed, mine), packed)
    coarse[...] = packed
    for k in range(5):
        free_out[k] = free[k + 3]
    for k in range(OWN):
        right_out[k] = right[k + 3]


def correct_kernel(
    slabs, info, smooth, dens, free, right, gathered, moved, image, passed, slope, sums, mod, x, d, w, target, p, own_mod, energy
):
    coarse_plane, plane, groups = Plane(4), Plane(1), Groups()
    slab, mirror, sweep_count = info[0], info[1], info[3]
    offset = slab % 4
    upper_rows = lax.broadcasted_iota(jnp.int32, (ROWS, COLS), 0) >= 4
    odd = groups.lane_bits[0]
    groups_of = [(k, ROWS) for k in range(4)] + [(k, 0) for k in range(4)] + [(4 + k, ROWS) for k in range(4)]

    def unpack(field, j):
        block, row = groups_of[j]
        first = gathered[block, row + field : row + field + 1]
        second = gathered[block, row + 4 + field : row + 5 + field]
        return jnp.where(upper_rows, jnp.broadcast_to(second, (ROWS, COLS)), jnp.broadcast_to(first, (ROWS, COLS)))

    for lead in range(4):

        @pl.when(offset == lead)
        def _(lead=lead):
            for q in range(9):
                mod[q] = unpack(3, lead + q)
            for c in range(3):
                lower = None
                for q in range(9):
                    value = unpack(c, lead + q)
                    if q > 0:
                        part = jnp.where(odd, pltpu.roll(value, 1, 1), value)
                        target[c, q - 1] = part + jnp.where(odd, lower, pltpu.roll(lower, COLS - 1, 1))
                    lower = value

    summed = coarse_plane.corner_sum(mod[0])
    for q in range(8):
        lower, summed = summed, coarse_plane.corner_sum(mod[q + 1])
        scaling = np.float32(4.0 * row_total()) * (lower + summed)
        at = slab - 3 + q
        inside = ((at >= 0) & (at < slabs)).astype(jnp.float32)
        inverse = inside / jnp.where(scaling > 0.0, scaling, 1.0)
        w[q] = inverse
        for c in range(3):
            start = target[c, q] * (inverse * np.float32(1.0 / CENTRE))
            x[c, q] = start
            d[c, q] = start

    for k, (keep, add) in enumerate(chebyshev_factors(), 1):

        @pl.when(k < sweep_count)
        def _(k=k, keep=keep, add=add):
            def consume(q, forces, _energy):
                weight = w[q] * np.float32(add)
                for c in range(3):
                    update = np.float32(keep) * d[c, q] + weight * (target[c, q] - forces[c])
                    d[c, q] = update
                    x[c, q] = x[c, q] + update

            apply_planes(
                coarse_plane,
                k - 1,
                7 - k,
                lambda q: [x[c, q] for c in range(3)],
                lambda q: mod[q + 1],
                4.0,
                consume,
            )

    half = pl.ds(pl.multiple_of(mirror * 128, 128), 128)
    for k in range(5):
        for c in range(3):
            p[c, k] = smooth[c, k] + free[k] * x[c, 4 if k == 4 else 3]
    for k in range(OWN):
        own_mod[k] = modulus_of(dens[k])

    def consume_image(q, forces, strain):
        for c in range(3):
            x[c, q] = forces[c]
        energy[q] = strain

    def load_p(q):
        f = free[q]
        return [f * p[c, q] for c in range(3)]

    rest = apply_planes(plane, 0, 3, load_p, lambda q: own_mod[q], 1.0, consume_image, True)()

    first = jnp.zeros((ROWS, COLS), jnp.float32)
    second = jnp.zeros((ROWS, COLS), jnp.float32)
    for c in range(3):
        x[c, 4] = rest[c]
        passed[c] = x[c, 4, :, half]
    for k in range(OWN):
        second = second + own_mod[k] * energy[k]
        for c in range(3):
            value = p[c, k]
            first = first + (right[k] * np.float32(DIRECTION[c])) * value
            second = second + (1.0 - free[k]) * (value * value)
            moved[c, k] = p[c, k, :, half]
            image[c, k] = x[c, k, :, half]
        density = dens[k]
        energy[k] = np.float32(-3.0 * (1.0 - MODULUS_FLOOR)) * (density * density) * energy[k]
    turned = flipped(jnp.concatenate([energy[k, :, 128:] for k in range(OWN)], axis=0))
    for k in range(OWN):
        slope[k] = energy[k, :, :128] + turned[ROWS * k : ROWS * (k + 1)]
    lane = lax.broadcasted_iota(jnp.int32, (1, 128), 1)
    dots = jnp.where(lane == 0, jnp.sum(first), jnp.where(lane == 1, jnp.sum(second), 0.0))
    for k in range(sums.shape[0]):
        sums[k] = dots


def scale_kernel(totals, load, fixed, moved, image, arrived, slope, displacement, residual, sensitivity):
    total = totals[0]
    for k in range(1, totals.shape[0]):
        total = total + totals[k]
    lane = lax.broadcasted_iota(jnp.int32, (1, 128), 1)
    residual_dot = jnp.sum(jnp.where(lane == 0, total, 0.0), axis=1, keepdims=True)
    curvature = jnp.sum(jnp.where(lane == 1, total, 0.0), axis=1, keepdims=True)
    alpha = jnp.broadcast_to(residual_dot / curvature, (ROWS, 128))
    for k in range(OWN):
        loaded = ((1 - fixed[0, k]) * load[0, k]).astype(jnp.float32)
        for c in range(3):
            displacement[c, k] = alpha * moved[c, k]
            forces = image[c, k] + arrived[c] if k == 0 else image[c, k]
            forces = jnp.where(fixed[0, k] == 0, forces, moved[c, k])
            residual[c, k] = loaded * np.float32(DIRECTION[c]) - alpha * forces
        sensitivity[k] = alpha * (alpha * slope[k])


def call(kernel, outs, ins, scratch=()):
    vmem = pl.BlockSpec(memory_space=pltpu.VMEM)
    smem = pl.BlockSpec(memory_space=pltpu.SMEM)
    return pl.pallas_call(
        kernel,
        out_shape=[jax.ShapeDtypeStruct(shape, jnp.float32) for shape in outs],
        in_specs=[smem if v.ndim == 1 else vmem for v in ins],
        out_specs=[vmem] * len(outs),
        scratch_shapes=[pltpu.VMEM(shape, jnp.float32) for shape in scratch],
        compiler_params=pltpu.CompilerParams(vmem_limit_bytes=16 * 1024 * 1024),
    )(*ins)


def shifted(array, axis, by):
    length = lax.axis_size(axis)
    pairs = [(i, i + by) for i in range(length) if 0 <= i + by < length]
    return lax.ppermute(array, axis, pairs)


def run_smooth(slabs, info, own, below, above, masks):
    plane = (ROWS, COLS)
    field = (3, 11) + plane
    return call(
        functools.partial(smooth_kernel, slabs),
        [(3, 5) + plane, plane, (OWN,) + plane, (5,) + plane, (OWN,) + plane],
        [info, own, below, above, masks],
        [(12,) + plane, field, field, (11,) + plane, (11,) + plane, (11,) + plane, (3, 4) + plane],
    )


def run_correct(slabs, group, info, smooth, dens, free, right, gathered):
    plane = (ROWS, COLS)
    field = (3, 8) + plane
    part = (3, OWN, ROWS, 128)
    return call(
        functools.partial(correct_kernel, slabs),
        [part, part, (3, ROWS, 128), part[1:], (group, 1, 128)],
        [info, smooth, dens, free, right, gathered],
        [(9,) + plane, field, field, (8,) + plane, field, (3, 5) + plane, (OWN,) + plane, (OWN,) + plane],
    )


def on_device(density, load_mask, fixed_mask, sweeps):
    slabs = lax.axis_size(SLAB)
    slab, mirror = lax.axis_index(SLAB), lax.axis_index("mirror")
    info = jnp.concatenate([jnp.stack([slab, mirror]).astype(jnp.int32), sweeps])

    (own,) = call(pack_kernel, [(3,) + density.shape], [density, load_mask, fixed_mask])
    below = shifted(own, SLAB, 1)
    above = shifted(own, SLAB, -1)
    masks = lax.all_gather(jnp.concatenate([below[1:], own[1:], above[1:]], axis=0), "mirror")
    masks = masks.reshape((12,) + density.shape)
    smooth, coarse, dens, free, right = run_smooth(slabs, info, own, below, above, masks)

    reach = 4
    pairs = [(i, i + reach) for i in range(slabs - reach)]
    pairs += [(slabs + i + reach, slabs + i) for i in range(slabs - reach)]
    arrived = lax.ppermute(coarse, ("mirror",) + SLAB, pairs)
    sent = jnp.broadcast_to(jnp.concatenate([coarse, arrived], axis=0), (8, 2 * ROWS, COLS))
    gathered = lax.all_to_all(sent, ("mirror", "x"), 0, 0)

    part = (3, OWN, ROWS, 128)
    group = lax.axis_size(("y", "x"))
    moved, image, passed, slope, sums = run_correct(slabs, group, info, smooth, dens, free, right, gathered)
    added = shifted(passed, SLAB, 1)
    sums = lax.all_to_all(sums, ("y", "x"), 0, 0)
    length = lax.axis_size("z")
    sums = jnp.broadcast_to(jnp.sum(sums, axis=0), (length, 1, 128))
    sums = lax.all_to_all(sums, "z", 0, 0)
    displacement, residual, sensitivity = call(
        scale_kernel, [part, part, part[1:]], [sums, load_mask, fixed_mask, moved, image, added, slope]
    )
    return displacement[None], residual[None], sensitivity


def solution(mesh):
    slabs = mesh.shape["slab"]
    ways = 4
    deep = min(16, slabs // ways)
    split = Mesh(mesh.devices.reshape(2, slabs // (ways * deep), deep, ways), ("mirror",) + SLAB)
    return jax.shard_map(
        on_device,
        mesh=split,
        in_specs=(
            P(SLAB, None, None),
            P("mirror", SLAB, None, None),
            P("mirror", SLAB, None, None),
            P(),
        ),
        out_specs=(
            P("mirror", None, SLAB, None, None),
            P("mirror", None, SLAB, None, None),
            P(SLAB, None, None),
        ),
        check_vma=False,
    )
```

```python
import functools

import jax
import jax.numpy as jnp
import numpy as np
from jax import lax
from jax.experimental import pallas as pl
from jax.experimental.pallas import tpu as pltpu
from jax.sharding import Mesh
from jax.sharding import PartitionSpec as P

SWEEPS = 4
MODULUS_FLOOR = 0.001
EIG_LOWER = 0.05
EIG_UPPER = 1.0
CENTRE = 0.5 * (EIG_UPPER + EIG_LOWER)
HALF_WIDTH = 0.5 * (EIG_UPPER - EIG_LOWER)
DIRECTION = (0.4, -0.3, -1.0)
SLAB = ("y", "z", "x")
ROWS = 8
COLS = 256
OWN = 4
DENSITY, LOAD, FIXED, FIELDS = 0, 1, 2, 3


def element_matrix():
    poisson = 0.3
    lame_first = poisson / ((1.0 + poisson) * (1.0 - 2.0 * poisson))
    shear_modulus = 0.5 / (1.0 + poisson)
    elastic = np.zeros((6, 6))
    elastic[:3, :3] = lame_first
    for i in range(3):
        elastic[i, i] += 2.0 * shear_modulus
        elastic[i + 3, i + 3] = shear_modulus
    points = [0.5 - 0.5 / np.sqrt(3.0), 0.5 + 0.5 / np.sqrt(3.0)]
    stiffness = np.zeros((24, 24))
    for p in points:
        for q in points:
            for s in points:
                strain = np.zeros((6, 24))
                for corner in range(8):
                    z_bit, y_bit, x_bit = (corner // 4, corner // 2 % 2, corner % 2)
                    weight_z = p if z_bit else 1.0 - p
                    weight_y = q if y_bit else 1.0 - q
                    weight_x = s if x_bit else 1.0 - s
                    slope_z = 1.0 if z_bit else -1.0
                    slope_y = 1.0 if y_bit else -1.0
                    slope_x = 1.0 if x_bit else -1.0
                    grad_x = slope_x * weight_y * weight_z
                    grad_y = weight_x * slope_y * weight_z
                    grad_z = weight_x * weight_y * slope_z
                    c = 3 * corner
                    strain[0, c] = grad_x
                    strain[1, c + 1] = grad_y
                    strain[2, c + 2] = grad_z
                    strain[3, c] = grad_y
                    strain[3, c + 1] = grad_x
                    strain[4, c + 1] = grad_z
                    strain[4, c + 2] = grad_y
                    strain[5, c] = grad_z
                    strain[5, c + 2] = grad_x
                stiffness += strain.T @ elastic @ strain / 8.0
    return stiffness


@functools.lru_cache(None)
def mode_matrix():
    one = np.array([[1.0, 1.0], [-1.0, 1.0]])
    signs = np.kron(np.kron(one, one), one)
    spread = np.kron(signs, np.eye(3)) / 8.0
    matrix = spread @ element_matrix() @ spread.T
    table = {}
    for row in range(24):
        entries = [
            ((col // 3, col % 3), float(matrix[row, col]))
            for col in range(24)
            if abs(matrix[row, col]) > 1e-12
        ]
        if entries:
            table[(row // 3, row % 3)] = entries
    return table


@functools.lru_cache(None)
def row_total():
    totals = np.abs(element_matrix()).sum(axis=1)
    assert np.allclose(totals, totals[0], rtol=1e-12)
    return float(totals[0])


def chebyshev_factors():
    ratio = CENTRE / HALF_WIDTH
    rho = 1.0 / ratio
    factors = []
    for _ in range(1, SWEEPS):
        rho_next = 1.0 / (2.0 * ratio - rho)
        factors.append((rho_next * rho, 2.0 * rho_next / HALF_WIDTH))
        rho = rho_next
    return factors


class Plane:
    def __init__(self, step):
        lane = lax.broadcasted_iota(jnp.int32, (ROWS, COLS), 1)
        row = lax.broadcasted_iota(jnp.int32, (ROWS, COLS), 0)
        self.step = step
        self.lane_not_last = lane < COLS - step
        self.lane_not_first = lane >= step
        self.row_not_last = row < ROWS - step
        self.row_not_first = row >= step

    def next_x(self, v):
        return jnp.where(self.lane_not_last, pltpu.roll(v, COLS - self.step, 1), 0.0)

    def prev_x(self, v):
        return jnp.where(self.lane_not_first, pltpu.roll(v, self.step, 1), 0.0)

    def next_y(self, v):
        return jnp.where(self.row_not_last, pltpu.roll(v, ROWS - self.step, 0), 0.0)

    def prev_y(self, v):
        return jnp.where(self.row_not_first, pltpu.roll(v, self.step, 0), 0.0)

    def corner_sum(self, v):
        v = v + self.prev_x(v)
        return v + self.prev_y(v)

    def forward(self, comps):
        modes = [[None] * 3 for _ in range(4)]
        for c, v in enumerate(comps):
            ahead = self.next_x(v)
            for x_bit, w in enumerate((ahead + v, ahead - v)):
                above = self.next_y(w)
                modes[x_bit][c] = above + w
                modes[2 + x_bit][c] = above - w
        return modes

    def backward(self, modes):
        comps = []
        for c in range(3):
            along = []
            for x_bit in range(2):
                total, change = modes[x_bit][c], modes[2 + x_bit][c]
                along.append((total - change) + self.prev_y(total + change))
            comps.append((along[0] - along[1]) + self.prev_x(along[0] + along[1]))
        return comps

    def element(self, low, high, modulus, scale, with_energy=False):
        modes = {}
        for m in range(4):
            for c in range(3):
                if m > 0:
                    modes[(m, c)] = high[m][c] + low[m][c]
                modes[(4 + m, c)] = high[m][c] - low[m][c]
        forces = {}
        for row, entries in mode_matrix().items():
            total = None
            for col, entry in entries:
                term = modes[col] * np.float32(entry * scale)
                total = term if total is None else total + term
            forces[row] = total
        energy = None
        if with_energy:
            for row, force in forces.items():
                term = modes[row] * force
                energy = term if energy is None else energy + term
        on_low = [[None] * 3 for _ in range(4)]
        on_high = [[None] * 3 for _ in range(4)]
        for m in range(4):
            for c in range(3):
                change = modulus * forces[(4 + m, c)]
                if m > 0:
                    total = modulus * forces[(m, c)]
                    on_low[m][c] = total - change
                    on_high[m][c] = total + change
                else:
                    on_low[m][c] = -change
                    on_high[m][c] = change
        return on_low, on_high, energy


def apply_planes(plane, first, last, load, modulus_at, scale, consume, with_energy=False):
    def flat(modes):
        return tuple(v for mode in modes for v in mode)

    def nested(values):
        return [[values[3 * m + c] for c in range(3)] for m in range(4)]

    def body(q, carry):
        low, pending = nested(carry[:12]), nested(carry[12:])
        high = plane.forward(load(q + 1))
        on_low, on_high, energy = plane.element(low, high, modulus_at(q), scale, with_energy)
        total = [[pending[m][c] + on_low[m][c] for c in range(3)] for m in range(4)]
        consume(q, plane.backward(total), energy)
        return flat(high) + flat(on_high)

    start = flat(plane.forward(load(first)))
    zeros = tuple(jnp.zeros((ROWS, COLS), jnp.float32) for _ in range(12))
    carry = lax.fori_loop(first, last + 1, body, start + zeros, unroll=True)
    return lambda: plane.backward(nested(carry[12:]))


class Groups:
    def __init__(self):
        lane = lax.broadcasted_iota(jnp.int32, (ROWS, COLS), 1)
        row = lax.broadcasted_iota(jnp.int32, (ROWS, COLS), 0)
        self.lane_in, self.row_in = lane % 4, row % 4
        self.lane_bits = [lane % 2 == 1, lane // 2 % 2 == 1]
        self.row_bits = [row % 2 == 1, row // 2 % 2 == 1]

    def over_rows(self, v):
        for bit in range(2):
            by = 1 << bit
            v = v + jnp.where(self.row_bits[bit], pltpu.roll(v, by, 0), pltpu.roll(v, ROWS - by, 0))
        return v

    def over_lanes(self, v):
        for bit in range(2):
            by = 1 << bit
            v = v + jnp.where(self.lane_bits[bit], pltpu.roll(v, by, 1), pltpu.roll(v, COLS - by, 1))
        return v

    def both(self, v):
        return self.over_lanes(self.over_rows(v))


def modulus_of(density):
    return MODULUS_FLOOR + density * density * density * (1.0 - MODULUS_FLOOR)


def flip_matrix():
    row = lax.broadcasted_iota(jnp.int32, (128, 128), 0)
    return (row + lax.broadcasted_iota(jnp.int32, (128, 128), 1) == 127).astype(jnp.float32)


def flipped(stacked):
    return jnp.dot(stacked, flip_matrix(), precision=lax.Precision.HIGHEST, preferred_element_type=jnp.float32)


def both_halves(source, field, k):
    return jnp.concatenate([source[field, k], source[FIELDS + field, k]], axis=1)


def smooth_kernel(
    slabs, info, own, below, above, smooth, coarse, dens_out, free_out, right_out, mod, x, d, w, right, free, left
):
    plane, groups = Plane(1), Groups()
    slab, sweep_count = info[0], info[2]
    has_below = (slab > 0).astype(jnp.float32)
    has_above = (slab < slabs - 1).astype(jnp.float32)

    places = [(below, k, has_below) for k in range(OWN)]
    places += [(own, k, None) for k in range(OWN)]
    places += [(above, k, has_above) for k in range(OWN)]
    turned = flipped(jnp.concatenate([source[DENSITY, k] for source, k, _ in places], axis=0))
    for e, (source, k, inside) in enumerate(places):
        density = jnp.concatenate([source[DENSITY, k], turned[ROWS * e : ROWS * (e + 1)]], axis=1)
        value = modulus_of(density)
        mod[e] = value if inside is None else value * inside
        if source is own:
            dens_out[k] = density
        if e > 0:
            open_node = 1.0 - both_halves(source, FIXED, k)
            free[e - 1] = open_node if inside is None else open_node * inside

    summed = plane.corner_sum(mod[0])
    for q, (source, k, _) in enumerate(places[1:]):
        lower, summed = summed, plane.corner_sum(mod[q + 1])
        scaling = np.float32(row_total()) * (lower + summed)
        inverse = 1.0 / jnp.where(free[q] > 0.0, scaling, 1.0)
        w[q] = inverse
        loaded = free[q] * both_halves(source, LOAD, k)
        right[q] = loaded
        start = loaded * (inverse * np.float32(1.0 / CENTRE))
        for c in range(3):
            x[c, q] = start * np.float32(DIRECTION[c])
            d[c, q] = start * np.float32(DIRECTION[c])

    def load(q):
        f = free[q]
        return [f * x[c, q] for c in range(3)]

    def modulus_at(q):
        return mod[q + 1]

    for k, (keep, add) in enumerate(chebyshev_factors(), 1):

        @pl.when(k < sweep_count)
        def _(k=k, keep=keep, add=add):
            def consume(q, forces, _energy):
                f, weight = free[q], w[q] * np.float32(add)
                is_free = f > 0.0
                loaded = right[q]
                for c in range(3):
                    now = x[c, q]
                    image = jnp.where(is_free, forces[c], now)
                    defect = loaded * np.float32(DIRECTION[c]) - image
                    update = np.float32(keep) * d[c, q] + weight * defect
                    d[c, q] = update
                    x[c, q] = now + update

            apply_planes(plane, k - 1, 10 - k, load, modulus_at, 1.0, consume)

    def consume_left(q, forces, _energy):
        is_free = free[q] > 0.0
        for c in range(3):
            image = jnp.where(is_free, forces[c], x[c, q])
            left[c, q - 3] = right[q] * np.float32(DIRECTION[c]) - image

    rest = apply_planes(plane, 3, 6, load, modulus_at, 1.0, consume_left)()

    odd = groups.lane_bits[0]
    packed = groups.both((mod[4] + mod[5]) + (mod[6] + mod[7])) * np.float32(1.0 / 64.0)
    for c in range(3):
        for k in range(5):
            smooth[c, k] = x[c, k + 3]
        mine = groups.both((left[c, 0] + left[c, 1]) + (left[c, 2] + left[c, 3]))
        passed = groups.both(free[7] * -rest[c])
        packed = jnp.where(groups.row_in == c, jnp.where(odd, passed, mine), packed)
    coarse[...] = packed
    for k in range(5):
        free_out[k] = free[k + 3]
    for k in range(OWN):
        right_out[k] = right[k + 3]


def correct_kernel(
    slabs, info, smooth, dens, free, right, gathered, moved, image, passed, slope, sums, mod, x, d, w, target, p, own_mod, energy
):
    coarse_plane, plane, groups = Plane(4), Plane(1), Groups()
    slab, mirror, sweep_count = info[0], info[1], info[3]
    offset = slab % 4
    upper_rows = lax.broadcasted_iota(jnp.int32, (ROWS, COLS), 0) >= 4
    odd = groups.lane_bits[0]
    groups_of = [(k, ROWS) for k in range(4)] + [(k, 0) for k in range(4)] + [(4 + k, ROWS) for k in range(4)]

    def unpack(field, j):
        block, row = groups_of[j]
        first = gathered[block, row + field : row + field + 1]
        second = gathered[block, row + 4 + field : row + 5 + field]
        return jnp.where(upper_rows, jnp.broadcast_to(second, (ROWS, COLS)), jnp.broadcast_to(first, (ROWS, COLS)))

    for lead in range(4):

        @pl.when(offset == lead)
        def _(lead=lead):
            for q in range(9):
                mod[q] = unpack(3, lead + q)
            for c in range(3):
                lower = None
                for q in range(9):
                    value = unpack(c, lead + q)
                    if q > 0:
                        part = jnp.where(odd, pltpu.roll(value, 1, 1), value)
                        target[c, q - 1] = part + jnp.where(odd, lower, pltpu.roll(lower, COLS - 1, 1))
                    lower = value

    summed = coarse_plane.corner_sum(mod[0])
    for q in range(8):
        lower, summed = summed, coarse_plane.corner_sum(mod[q + 1])
        scaling = np.float32(4.0 * row_total()) * (lower + summed)
        at = slab - 3 + q
        inside = ((at >= 0) & (at < slabs)).astype(jnp.float32)
        inverse = inside / jnp.where(scaling > 0.0, scaling, 1.0)
        w[q] = inverse
        for c in range(3):
            start = target[c, q] * (inverse * np.float32(1.0 / CENTRE))
            x[c, q] = start
            d[c, q] = start

    for k, (keep, add) in enumerate(chebyshev_factors(), 1):

        @pl.when(k < sweep_count)
        def _(k=k, keep=keep, add=add):
            def consume(q, forces, _energy):
                weight = w[q] * np.float32(add)
                for c in range(3):
                    update = np.float32(keep) * d[c, q] + weight * (target[c, q] - forces[c])
                    d[c, q] = update
                    x[c, q] = x[c, q] + update

            apply_planes(
                coarse_plane,
                k - 1,
                7 - k,
                lambda q: [x[c, q] for c in range(3)],
                lambda q: mod[q + 1],
                4.0,
                consume,
            )

    half = pl.ds(pl.multiple_of(mirror * 128, 128), 128)
    for k in range(5):
        for c in range(3):
            p[c, k] = smooth[c, k] + free[k] * x[c, 4 if k == 4 else 3]
    for k in range(OWN):
        own_mod[k] = modulus_of(dens[k])

    def consume_image(q, forces, strain):
        for c in range(3):
            x[c, q] = forces[c]
        energy[q] = strain

    def load_p(q):
        f = free[q]
        return [f * p[c, q] for c in range(3)]

    rest = apply_planes(plane, 0, 3, load_p, lambda q: own_mod[q], 1.0, consume_image, True)()

    first = jnp.zeros((ROWS, COLS), jnp.float32)
    second = jnp.zeros((ROWS, COLS), jnp.float32)
    for c in range(3):
        x[c, 4] = rest[c]
        passed[c] = x[c, 4, :, half]
    for k in range(OWN):
        second = second + own_mod[k] * energy[k]
        for c in range(3):
            value = p[c, k]
            first = first + (right[k] * np.float32(DIRECTION[c])) * value
            second = second + (1.0 - free[k]) * (value * value)
            moved[c, k] = p[c, k, :, half]
            image[c, k] = x[c, k, :, half]
        density = dens[k]
        energy[k] = np.float32(-3.0 * (1.0 - MODULUS_FLOOR)) * (density * density) * energy[k]
    turned = flipped(jnp.concatenate([energy[k, :, 128:] for k in range(OWN)], axis=0))
    for k in range(OWN):
        slope[k] = energy[k, :, :128] + turned[ROWS * k : ROWS * (k + 1)]
    lane = lax.broadcasted_iota(jnp.int32, (1, 128), 1)
    dots = jnp.where(lane == 0, jnp.sum(first), jnp.where(lane == 1, jnp.sum(second), 0.0))
    for k in range(sums.shape[0]):
        sums[k] = dots


def scale_kernel(totals, load, fixed, moved, image, arrived, slope, displacement, residual, sensitivity):
    total = totals[0]
    for k in range(1, totals.shape[0]):
        total = total + totals[k]
    lane = lax.broadcasted_iota(jnp.int32, (1, 128), 1)
    residual_dot = jnp.sum(jnp.where(lane == 0, total, 0.0), axis=1, keepdims=True)
    curvature = jnp.sum(jnp.where(lane == 1, total, 0.0), axis=1, keepdims=True)
    alpha = jnp.broadcast_to(residual_dot / curvature, (ROWS, 128))
    for k in range(OWN):
        loaded = ((1 - fixed[0, k]) * load[0, k]).astype(jnp.float32)
        for c in range(3):
            displacement[c, k] = alpha * moved[c, k]
            forces = image[c, k] + arrived[c] if k == 0 else image[c, k]
            forces = jnp.where(fixed[0, k] == 0, forces, moved[c, k])
            residual[c, k] = loaded * np.float32(DIRECTION[c]) - alpha * forces
        sensitivity[k] = alpha * (alpha * slope[k])


def call(kernel, outs, ins, scratch=()):
    vmem = pl.BlockSpec(memory_space=pltpu.VMEM)
    smem = pl.BlockSpec(memory_space=pltpu.SMEM)
    return pl.pallas_call(
        kernel,
        out_shape=[jax.ShapeDtypeStruct(shape, jnp.float32) for shape in outs],
        in_specs=[smem if v.ndim == 1 else vmem for v in ins],
        out_specs=[vmem] * len(outs),
        scratch_shapes=[pltpu.VMEM(shape, jnp.float32) for shape in scratch],
        compiler_params=pltpu.CompilerParams(vmem_limit_bytes=16 * 1024 * 1024),
    )(*ins)


def shifted(array, axis, by):
    length = lax.axis_size(axis)
    pairs = [(i, i + by) for i in range(length) if 0 <= i + by < length]
    return lax.ppermute(array, axis, pairs)


def run_smooth(slabs, info, own, below, above):
    plane = (ROWS, COLS)
    field = (3, 11) + plane
    return call(
        functools.partial(smooth_kernel, slabs),
        [(3, 5) + plane, plane, (OWN,) + plane, (5,) + plane, (OWN,) + plane],
        [info, own, below, above],
        [(12,) + plane, field, field, (11,) + plane, (11,) + plane, (11,) + plane, (3, 4) + plane],
    )


def run_correct(slabs, group, info, smooth, dens, free, right, gathered):
    plane = (ROWS, COLS)
    field = (3, 8) + plane
    part = (3, OWN, ROWS, 128)
    return call(
        functools.partial(correct_kernel, slabs),
        [part, part, (3, ROWS, 128), part[1:], (group, 1, 128)],
        [info, smooth, dens, free, right, gathered],
        [(9,) + plane, field, field, (8,) + plane, field, (3, 5) + plane, (OWN,) + plane, (OWN,) + plane],
    )


def on_device(density, load_mask, fixed_mask, sweeps):
    slabs = lax.axis_size(SLAB)
    slab, mirror = lax.axis_index(SLAB), lax.axis_index("mirror")
    info = jnp.concatenate([jnp.stack([slab, mirror]).astype(jnp.int32), sweeps])

    here = jnp.concatenate([density[None], load_mask.astype(jnp.float32), fixed_mask.astype(jnp.float32)], axis=0)
    own = lax.all_gather(here, "mirror").reshape((2 * FIELDS,) + density.shape)
    near = [(i, i + 1) for i in range(slabs - 1)]
    near += [(slabs + i + 1, slabs + i) for i in range(slabs - 1)]
    both = lax.all_gather(lax.ppermute(own, ("mirror",) + SLAB, near), "mirror")
    below, above = both[0], both[1]
    smooth, coarse, dens, free, right = run_smooth(slabs, info, own, below, above)

    reach = 4
    pairs = [(i, i + reach) for i in range(slabs - reach)]
    pairs += [(slabs + i + reach, slabs + i) for i in range(slabs - reach)]
    arrived = lax.ppermute(coarse, ("mirror",) + SLAB, pairs)
    sent = jnp.broadcast_to(jnp.concatenate([coarse, arrived], axis=0), (8, 2 * ROWS, COLS))
    gathered = lax.all_to_all(sent, ("mirror", "x"), 0, 0)

    part = (3, OWN, ROWS, 128)
    group = lax.axis_size(("y", "x"))
    moved, image, passed, slope, sums = run_correct(slabs, group, info, smooth, dens, free, right, gathered)
    added = shifted(passed, SLAB, 1)
    sums = lax.all_to_all(sums, ("y", "x"), 0, 0)
    length = lax.axis_size("z")
    sums = jnp.broadcast_to(jnp.sum(sums, axis=0), (length, 1, 128))
    sums = lax.all_to_all(sums, "z", 0, 0)
    displacement, residual, sensitivity = call(
        scale_kernel, [part, part, part[1:]], [sums, load_mask, fixed_mask, moved, image, added, slope]
    )
    return displacement[None], residual[None], sensitivity


def solution(mesh):
    slabs = mesh.shape["slab"]
    ways = 4
    deep = min(16, slabs // ways)
    split = Mesh(mesh.devices.reshape(2, slabs // (ways * deep), deep, ways), ("mirror",) + SLAB)
    return jax.shard_map(
        on_device,
        mesh=split,
        in_specs=(
            P(SLAB, None, None),
            P("mirror", SLAB, None, None),
            P("mirror", SLAB, None, None),
            P(),
        ),
        out_specs=(
            P("mirror", None, SLAB, None, None),
            P("mirror", None, SLAB, None, None),
            P(SLAB, None, None),
        ),
        check_vma=False,
    )
```

```python
import functools

import jax
import jax.numpy as jnp
import numpy as np
from jax import lax
from jax.experimental import pallas as pl
from jax.experimental.pallas import tpu as pltpu
from jax.sharding import Mesh
from jax.sharding import PartitionSpec as P

SWEEPS = 4
MODULUS_FLOOR = 0.001
EIG_LOWER = 0.05
EIG_UPPER = 1.0
CENTRE = 0.5 * (EIG_UPPER + EIG_LOWER)
HALF_WIDTH = 0.5 * (EIG_UPPER - EIG_LOWER)
DIRECTION = (0.4, -0.3, -1.0)
SLAB = ("y", "z", "x")
ROWS = 8
COLS = 256
OWN = 4
DENSITY, LOAD, FIXED, FIELDS = 0, 1, 2, 3


def element_matrix():
    poisson = 0.3
    lame_first = poisson / ((1.0 + poisson) * (1.0 - 2.0 * poisson))
    shear_modulus = 0.5 / (1.0 + poisson)
    elastic = np.zeros((6, 6))
    elastic[:3, :3] = lame_first
    for i in range(3):
        elastic[i, i] += 2.0 * shear_modulus
        elastic[i + 3, i + 3] = shear_modulus
    points = [0.5 - 0.5 / np.sqrt(3.0), 0.5 + 0.5 / np.sqrt(3.0)]
    stiffness = np.zeros((24, 24))
    for p in points:
        for q in points:
            for s in points:
                strain = np.zeros((6, 24))
                for corner in range(8):
                    z_bit, y_bit, x_bit = (corner // 4, corner // 2 % 2, corner % 2)
                    weight_z = p if z_bit else 1.0 - p
                    weight_y = q if y_bit else 1.0 - q
                    weight_x = s if x_bit else 1.0 - s
                    slope_z = 1.0 if z_bit else -1.0
                    slope_y = 1.0 if y_bit else -1.0
                    slope_x = 1.0 if x_bit else -1.0
                    grad_x = slope_x * weight_y * weight_z
                    grad_y = weight_x * slope_y * weight_z
                    grad_z = weight_x * weight_y * slope_z
                    c = 3 * corner
                    strain[0, c] = grad_x
                    strain[1, c + 1] = grad_y
                    strain[2, c + 2] = grad_z
                    strain[3, c] = grad_y
                    strain[3, c + 1] = grad_x
                    strain[4, c + 1] = grad_z
                    strain[4, c + 2] = grad_y
                    strain[5, c] = grad_z
                    strain[5, c + 2] = grad_x
                stiffness += strain.T @ elastic @ strain / 8.0
    return stiffness


STRETCH = ((1, 0), (2, 1), (4, 2))
SHEAR = (((2, 0), (1, 1)), ((4, 0), (1, 2)), ((4, 1), (2, 2)))
BEND = (((5, 0), (6, 1)), ((3, 0), (6, 2)), ((3, 1), (5, 2)))
TWIST = ((6, 0), (5, 1), (3, 2))
WARP = ((7, 0), (7, 1), (7, 2))


@functools.lru_cache(None)
def mode_entries():
    one = np.array([[1.0, 1.0], [-1.0, 1.0]])
    signs = np.kron(np.kron(one, one), one)
    spread = np.kron(signs, np.eye(3)) / 8.0
    matrix = spread @ element_matrix() @ spread.T

    def at(row, col):
        return matrix[3 * row[0] + row[1], 3 * col[0] + col[1]]

    names = {
        "stretch": (at(STRETCH[0], STRETCH[0]), at(STRETCH[0], STRETCH[1])),
        "shear": at(SHEAR[0][0], SHEAR[0][1]),
        "bend": (at(BEND[0][0], BEND[0][0]), at(BEND[0][0], BEND[0][1])),
        "twist": at(TWIST[0], TWIST[1]),
        "warp": at(WARP[0], WARP[0]),
    }
    again = np.zeros((24, 24))

    def put(modes, diagonal, other):
        for row in modes:
            for col in modes:
                again[3 * row[0] + row[1], 3 * col[0] + col[1]] = diagonal if row == col else other

    put(STRETCH, *names["stretch"])
    put(TWIST, 2.0 * names["twist"], names["twist"])
    for pair in SHEAR:
        put(pair, names["shear"], names["shear"])
    for pair in BEND:
        put(pair, *names["bend"])
    for mode in WARP:
        put((mode,), names["warp"], 0.0)
    assert np.allclose(matrix, again, rtol=0.0, atol=1e-13)
    return names


def mode_forces(modes, scale):
    entries = mode_entries()
    forces = {}
    diagonal, other = entries["stretch"]
    shared = (modes[STRETCH[0]] + modes[STRETCH[1]] + modes[STRETCH[2]]) * np.float32(other * scale)
    for mode in STRETCH:
        forces[mode] = shared + modes[mode] * np.float32((diagonal - other) * scale)
    for first, second in SHEAR:
        forces[first] = forces[second] = (modes[first] + modes[second]) * np.float32(entries["shear"] * scale)
    diagonal, other = np.float32(entries["bend"][0] * scale), np.float32(entries["bend"][1] * scale)
    for first, second in BEND:
        forces[first] = modes[first] * diagonal + modes[second] * other
        forces[second] = modes[second] * diagonal + modes[first] * other
    shared = modes[TWIST[0]] + modes[TWIST[1]] + modes[TWIST[2]]
    for mode in TWIST:
        forces[mode] = (shared + modes[mode]) * np.float32(entries["twist"] * scale)
    for mode in WARP:
        forces[mode] = modes[mode] * np.float32(entries["warp"] * scale)
    return forces


@functools.lru_cache(None)
def row_total():
    totals = np.abs(element_matrix()).sum(axis=1)
    assert np.allclose(totals, totals[0], rtol=1e-12)
    return float(totals[0])


def chebyshev_factors():
    ratio = CENTRE / HALF_WIDTH
    rho = 1.0 / ratio
    factors = []
    for _ in range(1, SWEEPS):
        rho_next = 1.0 / (2.0 * ratio - rho)
        factors.append((rho_next * rho, 2.0 * rho_next / HALF_WIDTH))
        rho = rho_next
    return factors


class Plane:
    def __init__(self, step):
        lane = lax.broadcasted_iota(jnp.int32, (ROWS, COLS), 1)
        row = lax.broadcasted_iota(jnp.int32, (ROWS, COLS), 0)
        self.step = step
        self.lane_not_last = lane < COLS - step
        self.lane_not_first = lane >= step
        self.row_not_last = row < ROWS - step
        self.row_not_first = row >= step

    def next_x(self, v):
        return jnp.where(self.lane_not_last, pltpu.roll(v, COLS - self.step, 1), 0.0)

    def prev_x(self, v):
        return jnp.where(self.lane_not_first, pltpu.roll(v, self.step, 1), 0.0)

    def next_y(self, v):
        return jnp.where(self.row_not_last, pltpu.roll(v, ROWS - self.step, 0), 0.0)

    def prev_y(self, v):
        return jnp.where(self.row_not_first, pltpu.roll(v, self.step, 0), 0.0)

    def corner_sum(self, v):
        v = v + self.prev_x(v)
        return v + self.prev_y(v)

    def forward(self, comps):
        modes = [[None] * 3 for _ in range(4)]
        for c, v in enumerate(comps):
            ahead = self.next_x(v)
            for x_bit, w in enumerate((ahead + v, ahead - v)):
                above = self.next_y(w)
                modes[x_bit][c] = above + w
                modes[2 + x_bit][c] = above - w
        return modes

    def backward(self, modes):
        comps = []
        for c in range(3):
            along = []
            for x_bit in range(2):
                total, change = modes[x_bit][c], modes[2 + x_bit][c]
                along.append((total - change) + self.prev_y(total + change))
            comps.append((along[0] - along[1]) + self.prev_x(along[0] + along[1]))
        return comps

    def element(self, low, high, modulus, scale, with_energy=False):
        modes = {}
        for m in range(4):
            for c in range(3):
                if m > 0:
                    modes[(m, c)] = high[m][c] + low[m][c]
                modes[(4 + m, c)] = high[m][c] - low[m][c]
        forces = mode_forces(modes, scale)
        energy = None
        if with_energy:
            terms = [forces[first] * (modes[first] + modes[second]) for first, second in SHEAR]
            paired = [mode for pair in SHEAR for mode in pair]
            terms += [forces[mode] * modes[mode] for mode in forces if mode not in paired]
            for term in terms:
                energy = term if energy is None else energy + term
        for first, second in SHEAR:
            forces[first] = forces[second] = modulus * forces[first]
        for mode in STRETCH + TWIST + WARP + BEND[0] + BEND[1] + BEND[2]:
            forces[mode] = modulus * forces[mode]
        on_low = [[None] * 3 for _ in range(4)]
        on_high = [[None] * 3 for _ in range(4)]
        for m in range(4):
            for c in range(3):
                change = forces[(4 + m, c)]
                if m > 0:
                    total = forces[(m, c)]
                    on_low[m][c] = total - change
                    on_high[m][c] = total + change
                else:
                    on_low[m][c] = -change
                    on_high[m][c] = change
        return on_low, on_high, energy


def apply_planes(plane, first, last, load, modulus_at, scale, consume, with_energy=False):
    def flat(modes):
        return tuple(v for mode in modes for v in mode)

    def nested(values):
        return [[values[3 * m + c] for c in range(3)] for m in range(4)]

    def body(q, carry):
        low, pending = nested(carry[:12]), nested(carry[12:])
        high = plane.forward(load(q + 1))
        on_low, on_high, energy = plane.element(low, high, modulus_at(q), scale, with_energy)
        total = [[pending[m][c] + on_low[m][c] for c in range(3)] for m in range(4)]
        consume(q, plane.backward(total), energy)
        return flat(high) + flat(on_high)

    start = flat(plane.forward(load(first)))
    zeros = tuple(jnp.zeros((ROWS, COLS), jnp.float32) for _ in range(12))
    carry = lax.fori_loop(first, last + 1, body, start + zeros, unroll=True)
    return lambda: plane.backward(nested(carry[12:]))


class Groups:
    def __init__(self):
        lane = lax.broadcasted_iota(jnp.int32, (ROWS, COLS), 1)
        row = lax.broadcasted_iota(jnp.int32, (ROWS, COLS), 0)
        self.lane_in, self.row_in = lane % 4, row % 4
        self.lane_bits = [lane % 2 == 1, lane // 2 % 2 == 1]
        self.row_bits = [row % 2 == 1, row // 2 % 2 == 1]

    def over_rows(self, v):
        for bit in range(2):
            by = 1 << bit
            v = v + jnp.where(self.row_bits[bit], pltpu.roll(v, by, 0), pltpu.roll(v, ROWS - by, 0))
        return v

    def over_lanes(self, v):
        for bit in range(2):
            by = 1 << bit
            v = v + jnp.where(self.lane_bits[bit], pltpu.roll(v, by, 1), pltpu.roll(v, COLS - by, 1))
        return v

    def both(self, v):
        return self.over_lanes(self.over_rows(v))


def modulus_of(density):
    return MODULUS_FLOOR + density * density * density * (1.0 - MODULUS_FLOOR)


def flip_matrix():
    row = lax.broadcasted_iota(jnp.int32, (128, 128), 0)
    return (row + lax.broadcasted_iota(jnp.int32, (128, 128), 1) == 127).astype(jnp.float32)


def flipped(stacked):
    return jnp.dot(stacked, flip_matrix(), precision=lax.Precision.HIGHEST, preferred_element_type=jnp.float32)


def both_halves(source, field, k):
    return jnp.concatenate([source[field, k], source[FIELDS + field, k]], axis=1)


def smooth_kernel(
    slabs, info, own, below, above, smooth, coarse, dens_out, free_out, right_out, mod, x, d, w, right, free, left
):
    plane, groups = Plane(1), Groups()
    slab, sweep_count = info[0], info[2]
    has_below = (slab > 0).astype(jnp.float32)
    has_above = (slab < slabs - 1).astype(jnp.float32)

    places = [(below, k, has_below) for k in range(OWN)]
    places += [(own, k, None) for k in range(OWN)]
    places += [(above, k, has_above) for k in range(OWN)]
    turned = flipped(jnp.concatenate([source[DENSITY, k] for source, k, _ in places], axis=0))
    for e, (source, k, inside) in enumerate(places):
        density = jnp.concatenate([source[DENSITY, k], turned[ROWS * e : ROWS * (e + 1)]], axis=1)
        value = modulus_of(density)
        mod[e] = value if inside is None else value * inside
        if source is own:
            dens_out[k] = density
        if e > 0:
            open_node = 1.0 - both_halves(source, FIXED, k)
            free[e - 1] = open_node if inside is None else open_node * inside

    summed = plane.corner_sum(mod[0])
    for q, (source, k, _) in enumerate(places[1:]):
        lower, summed = summed, plane.corner_sum(mod[q + 1])
        scaling = np.float32(row_total()) * (lower + summed)
        inverse = 1.0 / jnp.where(free[q] > 0.0, scaling, 1.0)
        w[q] = inverse
        loaded = free[q] * both_halves(source, LOAD, k)
        right[q] = loaded
        start = loaded * (inverse * np.float32(1.0 / CENTRE))
        for c in range(3):
            x[c, q] = start * np.float32(DIRECTION[c])
            d[c, q] = start * np.float32(DIRECTION[c])

    def load(q):
        f = free[q]
        return [f * x[c, q] for c in range(3)]

    def modulus_at(q):
        return mod[q + 1]

    for k, (keep, add) in enumerate(chebyshev_factors(), 1):

        @pl.when(k < sweep_count)
        def _(k=k, keep=keep, add=add):
            def consume(q, forces, _energy):
                f, weight = free[q], w[q] * np.float32(add)
                is_free = f > 0.0
                loaded = right[q]
                for c in range(3):
                    now = x[c, q]
                    image = jnp.where(is_free, forces[c], now)
                    defect = loaded * np.float32(DIRECTION[c]) - image
                    update = np.float32(keep) * d[c, q] + weight * defect
                    d[c, q] = update
                    x[c, q] = now + update

            apply_planes(plane, k - 1, 10 - k, load, modulus_at, 1.0, consume)

    def consume_left(q, forces, _energy):
        is_free = free[q] > 0.0
        for c in range(3):
            image = jnp.where(is_free, forces[c], x[c, q])
            left[c, q - 3] = right[q] * np.float32(DIRECTION[c]) - image

    rest = apply_planes(plane, 3, 6, load, modulus_at, 1.0, consume_left)()

    odd = groups.lane_bits[0]
    packed = groups.both((mod[4] + mod[5]) + (mod[6] + mod[7])) * np.float32(1.0 / 64.0)
    for c in range(3):
        for k in range(5):
            smooth[c, k] = x[c, k + 3]
        mine = groups.both((left[c, 0] + left[c, 1]) + (left[c, 2] + left[c, 3]))
        passed = groups.both(free[7] * -rest[c])
        packed = jnp.where(groups.row_in == c, jnp.where(odd, passed, mine), packed)
    coarse[...] = packed
    for k in range(5):
        free_out[k] = free[k + 3]
    for k in range(OWN):
        right_out[k] = right[k + 3]


def correct_kernel(
    slabs, info, smooth, dens, free, right, gathered, moved, image, passed, slope, sums, mod, x, d, w, target, p, own_mod, energy
):
    coarse_plane, plane, groups = Plane(4), Plane(1), Groups()
    slab, mirror, sweep_count = info[0], info[1], info[3]
    offset = slab % 4
    upper_rows = lax.broadcasted_iota(jnp.int32, (ROWS, COLS), 0) >= 4
    odd = groups.lane_bits[0]
    groups_of = [(k, ROWS) for k in range(4)] + [(k, 0) for k in range(4)] + [(4 + k, ROWS) for k in range(4)]

    def unpack(field, j):
        block, row = groups_of[j]
        first = gathered[block, row + field : row + field + 1]
        second = gathered[block, row + 4 + field : row + 5 + field]
        return jnp.where(upper_rows, jnp.broadcast_to(second, (ROWS, COLS)), jnp.broadcast_to(first, (ROWS, COLS)))

    for lead in range(4):

        @pl.when(offset == lead)
        def _(lead=lead):
            for q in range(9):
                mod[q] = unpack(3, lead + q)
            for c in range(3):
                lower = None
                for q in range(9):
                    value = unpack(c, lead + q)
                    if q > 0:
                        part = jnp.where(odd, pltpu.roll(value, 1, 1), value)
                        target[c, q - 1] = part + jnp.where(odd, lower, pltpu.roll(lower, COLS - 1, 1))
                    lower = value

    summed = coarse_plane.corner_sum(mod[0])
    for q in range(8):
        lower, summed = summed, coarse_plane.corner_sum(mod[q + 1])
        scaling = np.float32(4.0 * row_total()) * (lower + summed)
        at = slab - 3 + q
        inside = ((at >= 0) & (at < slabs)).astype(jnp.float32)
        inverse = inside / jnp.where(scaling > 0.0, scaling, 1.0)
        w[q] = inverse
        for c in range(3):
            start = target[c, q] * (inverse * np.float32(1.0 / CENTRE))
            x[c, q] = start
            d[c, q] = start

    for k, (keep, add) in enumerate(chebyshev_factors(), 1):

        @pl.when(k < sweep_count)
        def _(k=k, keep=keep, add=add):
            def consume(q, forces, _energy):
                weight = w[q] * np.float32(add)
                for c in range(3):
                    update = np.float32(keep) * d[c, q] + weight * (target[c, q] - forces[c])
                    d[c, q] = update
                    x[c, q] = x[c, q] + update

            apply_planes(
                coarse_plane,
                k - 1,
                7 - k,
                lambda q: [x[c, q] for c in range(3)],
                lambda q: mod[q + 1],
                4.0,
                consume,
            )

    half = pl.ds(pl.multiple_of(mirror * 128, 128), 128)
    for k in range(5):
        for c in range(3):
            p[c, k] = smooth[c, k] + free[k] * x[c, 4 if k == 4 else 3]
    for k in range(OWN):
        own_mod[k] = modulus_of(dens[k])

    def consume_image(q, forces, strain):
        for c in range(3):
            x[c, q] = forces[c]
        energy[q] = strain

    def load_p(q):
        f = free[q]
        return [f * p[c, q] for c in range(3)]

    rest = apply_planes(plane, 0, 3, load_p, lambda q: own_mod[q], 1.0, consume_image, True)()

    first = jnp.zeros((ROWS, COLS), jnp.float32)
    second = jnp.zeros((ROWS, COLS), jnp.float32)
    for c in range(3):
        x[c, 4] = rest[c]
        passed[c] = x[c, 4, :, half]
    for k in range(OWN):
        second = second + own_mod[k] * energy[k]
        for c in range(3):
            value = p[c, k]
            first = first + (right[k] * np.float32(DIRECTION[c])) * value
            second = second + (1.0 - free[k]) * (value * value)
            moved[c, k] = p[c, k, :, half]
            image[c, k] = x[c, k, :, half]
        density = dens[k]
        energy[k] = np.float32(-3.0 * (1.0 - MODULUS_FLOOR)) * (density * density) * energy[k]
    turned = flipped(jnp.concatenate([energy[k, :, 128:] for k in range(OWN)], axis=0))
    for k in range(OWN):
        slope[k] = energy[k, :, :128] + turned[ROWS * k : ROWS * (k + 1)]
    lane = lax.broadcasted_iota(jnp.int32, (1, 128), 1)
    dots = jnp.where(lane == 0, jnp.sum(first), jnp.where(lane == 1, jnp.sum(second), 0.0))
    for k in range(sums.shape[0]):
        sums[k] = dots


def scale_kernel(totals, load, fixed, moved, image, arrived, slope, displacement, residual, sensitivity):
    total = totals[0]
    for k in range(1, totals.shape[0]):
        total = total + totals[k]
    lane = lax.broadcasted_iota(jnp.int32, (1, 128), 1)
    residual_dot = jnp.sum(jnp.where(lane == 0, total, 0.0), axis=1, keepdims=True)
    curvature = jnp.sum(jnp.where(lane == 1, total, 0.0), axis=1, keepdims=True)
    alpha = jnp.broadcast_to(residual_dot / curvature, (ROWS, 128))
    for k in range(OWN):
        loaded = ((1 - fixed[0, k]) * load[0, k]).astype(jnp.float32)
        for c in range(3):
            displacement[c, k] = alpha * moved[c, k]
            forces = image[c, k] + arrived[c] if k == 0 else image[c, k]
            forces = jnp.where(fixed[0, k] == 0, forces, moved[c, k])
            residual[c, k] = loaded * np.float32(DIRECTION[c]) - alpha * forces
        sensitivity[k] = alpha * (alpha * slope[k])


def call(kernel, outs, ins, scratch=()):
    vmem = pl.BlockSpec(memory_space=pltpu.VMEM)
    smem = pl.BlockSpec(memory_space=pltpu.SMEM)
    return pl.pallas_call(
        kernel,
        out_shape=[jax.ShapeDtypeStruct(shape, jnp.float32) for shape in outs],
        in_specs=[smem if v.ndim == 1 else vmem for v in ins],
        out_specs=[vmem] * len(outs),
        scratch_shapes=[pltpu.VMEM(shape, jnp.float32) for shape in scratch],
        compiler_params=pltpu.CompilerParams(vmem_limit_bytes=16 * 1024 * 1024),
    )(*ins)


def shifted(array, axis, by):
    length = lax.axis_size(axis)
    pairs = [(i, i + by) for i in range(length) if 0 <= i + by < length]
    return lax.ppermute(array, axis, pairs)


def run_smooth(slabs, info, own, below, above):
    plane = (ROWS, COLS)
    field = (3, 11) + plane
    return call(
        functools.partial(smooth_kernel, slabs),
        [(3, 5) + plane, plane, (OWN,) + plane, (5,) + plane, (OWN,) + plane],
        [info, own, below, above],
        [(12,) + plane, field, field, (11,) + plane, (11,) + plane, (11,) + plane, (3, 4) + plane],
    )


def run_correct(slabs, group, info, smooth, dens, free, right, gathered):
    plane = (ROWS, COLS)
    field = (3, 8) + plane
    part = (3, OWN, ROWS, 128)
    return call(
        functools.partial(correct_kernel, slabs),
        [part, part, (3, ROWS, 128), part[1:], (group, 1, 128)],
        [info, smooth, dens, free, right, gathered],
        [(9,) + plane, field, field, (8,) + plane, field, (3, 5) + plane, (OWN,) + plane, (OWN,) + plane],
    )


def on_device(density, load_mask, fixed_mask, sweeps):
    slabs = lax.axis_size(SLAB)
    slab, mirror = lax.axis_index(SLAB), lax.axis_index("mirror")
    info = jnp.concatenate([jnp.stack([slab, mirror]).astype(jnp.int32), sweeps])

    here = jnp.concatenate([density[None], load_mask.astype(jnp.float32), fixed_mask.astype(jnp.float32)], axis=0)
    own = lax.all_gather(here, "mirror").reshape((2 * FIELDS,) + density.shape)
    near = [(i, i + 1) for i in range(slabs - 1)]
    near += [(slabs + i + 1, slabs + i) for i in range(slabs - 1)]
    both = lax.all_gather(lax.ppermute(own, ("mirror",) + SLAB, near), "mirror")
    below, above = both[0], both[1]
    smooth, coarse, dens, free, right = run_smooth(slabs, info, own, below, above)

    reach = 4
    pairs = [(i, i + reach) for i in range(slabs - reach)]
    pairs += [(slabs + i + reach, slabs + i) for i in range(slabs - reach)]
    arrived = lax.ppermute(coarse, ("mirror",) + SLAB, pairs)
    sent = jnp.broadcast_to(jnp.concatenate([coarse, arrived], axis=0), (8, 2 * ROWS, COLS))
    gathered = lax.all_to_all(sent, ("mirror", "x"), 0, 0)

    part = (3, OWN, ROWS, 128)
    group = lax.axis_size(("y", "x"))
    moved, image, passed, slope, sums = run_correct(slabs, group, info, smooth, dens, free, right, gathered)
    added = shifted(passed, SLAB, 1)
    sums = lax.all_to_all(sums, ("y", "x"), 0, 0)
    length = lax.axis_size("z")
    sums = jnp.broadcast_to(jnp.sum(sums, axis=0), (length, 1, 128))
    sums = lax.all_to_all(sums, "z", 0, 0)
    displacement, residual, sensitivity = call(
        scale_kernel, [part, part, part[1:]], [sums, load_mask, fixed_mask, moved, image, added, slope]
    )
    return displacement[None], residual[None], sensitivity


def solution(mesh):
    slabs = mesh.shape["slab"]
    ways = 4
    deep = min(16, slabs // ways)
    split = Mesh(mesh.devices.reshape(2, slabs // (ways * deep), deep, ways), ("mirror",) + SLAB)
    return jax.shard_map(
        on_device,
        mesh=split,
        in_specs=(
            P(SLAB, None, None),
            P("mirror", SLAB, None, None),
            P("mirror", SLAB, None, None),
            P(),
        ),
        out_specs=(
            P("mirror", None, SLAB, None, None),
            P("mirror", None, SLAB, None, None),
            P(SLAB, None, None),
        ),
        check_vma=False,
    )
```

```python
import functools

import jax
import jax.numpy as jnp
import numpy as np
from jax import lax
from jax.experimental import pallas as pl
from jax.experimental.pallas import tpu as pltpu
from jax.sharding import Mesh
from jax.sharding import PartitionSpec as P

SWEEPS = 4
MODULUS_FLOOR = 0.001
EIG_LOWER = 0.05
EIG_UPPER = 1.0
CENTRE = 0.5 * (EIG_UPPER + EIG_LOWER)
HALF_WIDTH = 0.5 * (EIG_UPPER - EIG_LOWER)
DIRECTION = (0.4, -0.3, -1.0)
SLAB = ("y", "z", "x")
ROWS = 8
COLS = 256
OWN = 4
DENSITY, LOAD, FIXED, FIELDS = 0, 1, 2, 3


def element_matrix():
    poisson = 0.3
    lame_first = poisson / ((1.0 + poisson) * (1.0 - 2.0 * poisson))
    shear_modulus = 0.5 / (1.0 + poisson)
    elastic = np.zeros((6, 6))
    elastic[:3, :3] = lame_first
    for i in range(3):
        elastic[i, i] += 2.0 * shear_modulus
        elastic[i + 3, i + 3] = shear_modulus
    points = [0.5 - 0.5 / np.sqrt(3.0), 0.5 + 0.5 / np.sqrt(3.0)]
    stiffness = np.zeros((24, 24))
    for p in points:
        for q in points:
            for s in points:
                strain = np.zeros((6, 24))
                for corner in range(8):
                    z_bit, y_bit, x_bit = (corner // 4, corner // 2 % 2, corner % 2)
                    weight_z = p if z_bit else 1.0 - p
                    weight_y = q if y_bit else 1.0 - q
                    weight_x = s if x_bit else 1.0 - s
                    slope_z = 1.0 if z_bit else -1.0
                    slope_y = 1.0 if y_bit else -1.0
                    slope_x = 1.0 if x_bit else -1.0
                    grad_x = slope_x * weight_y * weight_z
                    grad_y = weight_x * slope_y * weight_z
                    grad_z = weight_x * weight_y * slope_z
                    c = 3 * corner
                    strain[0, c] = grad_x
                    strain[1, c + 1] = grad_y
                    strain[2, c + 2] = grad_z
                    strain[3, c] = grad_y
                    strain[3, c + 1] = grad_x
                    strain[4, c + 1] = grad_z
                    strain[4, c + 2] = grad_y
                    strain[5, c] = grad_z
                    strain[5, c + 2] = grad_x
                stiffness += strain.T @ elastic @ strain / 8.0
    return stiffness


STRETCH = ((1, 0), (2, 1), (4, 2))
SHEAR = (((2, 0), (1, 1)), ((4, 0), (1, 2)), ((4, 1), (2, 2)))
BEND = (((5, 0), (6, 1)), ((3, 0), (6, 2)), ((3, 1), (5, 2)))
TWIST = ((6, 0), (5, 1), (3, 2))
WARP = ((7, 0), (7, 1), (7, 2))


@functools.lru_cache(None)
def mode_entries():
    one = np.array([[1.0, 1.0], [-1.0, 1.0]])
    signs = np.kron(np.kron(one, one), one)
    spread = np.kron(signs, np.eye(3)) / 8.0
    matrix = spread @ element_matrix() @ spread.T

    def at(row, col):
        return matrix[3 * row[0] + row[1], 3 * col[0] + col[1]]

    names = {
        "stretch": (at(STRETCH[0], STRETCH[0]), at(STRETCH[0], STRETCH[1])),
        "shear": at(SHEAR[0][0], SHEAR[0][1]),
        "bend": (at(BEND[0][0], BEND[0][0]), at(BEND[0][0], BEND[0][1])),
        "twist": at(TWIST[0], TWIST[1]),
        "warp": at(WARP[0], WARP[0]),
    }
    again = np.zeros((24, 24))

    def put(modes, diagonal, other):
        for row in modes:
            for col in modes:
                again[3 * row[0] + row[1], 3 * col[0] + col[1]] = diagonal if row == col else other

    put(STRETCH, *names["stretch"])
    put(TWIST, 2.0 * names["twist"], names["twist"])
    for pair in SHEAR:
        put(pair, names["shear"], names["shear"])
    for pair in BEND:
        put(pair, *names["bend"])
    for mode in WARP:
        put((mode,), names["warp"], 0.0)
    assert np.allclose(matrix, again, rtol=0.0, atol=1e-13)
    return names


def mode_forces(modes, scale):
    entries = mode_entries()
    forces = {}
    diagonal, other = entries["stretch"]
    shared = (modes[STRETCH[0]] + modes[STRETCH[1]] + modes[STRETCH[2]]) * np.float32(other * scale)
    for mode in STRETCH:
        forces[mode] = shared + modes[mode] * np.float32((diagonal - other) * scale)
    for first, second in SHEAR:
        forces[first] = forces[second] = (modes[first] + modes[second]) * np.float32(entries["shear"] * scale)
    diagonal, other = np.float32(entries["bend"][0] * scale), np.float32(entries["bend"][1] * scale)
    for first, second in BEND:
        forces[first] = modes[first] * diagonal + modes[second] * other
        forces[second] = modes[second] * diagonal + modes[first] * other
    shared = modes[TWIST[0]] + modes[TWIST[1]] + modes[TWIST[2]]
    for mode in TWIST:
        forces[mode] = (shared + modes[mode]) * np.float32(entries["twist"] * scale)
    for mode in WARP:
        forces[mode] = modes[mode] * np.float32(entries["warp"] * scale)
    return forces


def weighted_forces(modes, modulus, scale, with_energy):
    forces = mode_forces(modes, scale)
    energy = None
    if with_energy:
        terms = [forces[first] * (modes[first] + modes[second]) for first, second in SHEAR]
        paired = [mode for pair in SHEAR for mode in pair]
        terms += [forces[mode] * modes[mode] for mode in forces if mode not in paired]
        for term in terms:
            energy = term if energy is None else energy + term
    for first, second in SHEAR:
        forces[first] = forces[second] = modulus * forces[first]
    for mode in STRETCH + TWIST + WARP + BEND[0] + BEND[1] + BEND[2]:
        forces[mode] = modulus * forces[mode]
    return forces, energy


@functools.lru_cache(None)
def row_total():
    totals = np.abs(element_matrix()).sum(axis=1)
    assert np.allclose(totals, totals[0], rtol=1e-12)
    return float(totals[0])


def chebyshev_factors():
    ratio = CENTRE / HALF_WIDTH
    rho = 1.0 / ratio
    factors = []
    for _ in range(1, SWEEPS):
        rho_next = 1.0 / (2.0 * ratio - rho)
        factors.append((rho_next * rho, 2.0 * rho_next / HALF_WIDTH))
        rho = rho_next
    return factors


class Plane:
    def __init__(self, step):
        lane = lax.broadcasted_iota(jnp.int32, (ROWS, COLS), 1)
        row = lax.broadcasted_iota(jnp.int32, (ROWS, COLS), 0)
        self.step = step
        self.lane_not_last = lane < COLS - step
        self.lane_not_first = lane >= step
        self.row_not_last = row < ROWS - step
        self.row_not_first = row >= step

    def next_x(self, v):
        return jnp.where(self.lane_not_last, pltpu.roll(v, COLS - self.step, 1), 0.0)

    def prev_x(self, v):
        return jnp.where(self.lane_not_first, pltpu.roll(v, self.step, 1), 0.0)

    def next_y(self, v):
        return jnp.where(self.row_not_last, pltpu.roll(v, ROWS - self.step, 0), 0.0)

    def prev_y(self, v):
        return jnp.where(self.row_not_first, pltpu.roll(v, self.step, 0), 0.0)

    def corner_sum(self, v):
        v = v + self.prev_x(v)
        return v + self.prev_y(v)

    def forward(self, comps):
        modes = [[None] * 3 for _ in range(4)]
        for c, v in enumerate(comps):
            ahead = self.next_x(v)
            for x_bit, w in enumerate((ahead + v, ahead - v)):
                above = self.next_y(w)
                modes[x_bit][c] = above + w
                modes[2 + x_bit][c] = above - w
        return modes

    def backward(self, modes):
        comps = []
        for c in range(3):
            along = []
            for x_bit in range(2):
                total, change = modes[x_bit][c], modes[2 + x_bit][c]
                along.append((total - change) + self.prev_y(total + change))
            comps.append((along[0] - along[1]) + self.prev_x(along[0] + along[1]))
        return comps

    def element(self, low, high, modulus, scale, with_energy=False):
        modes = {}
        for m in range(4):
            for c in range(3):
                if m > 0:
                    modes[(m, c)] = high[m][c] + low[m][c]
                modes[(4 + m, c)] = high[m][c] - low[m][c]
        forces, energy = weighted_forces(modes, modulus, scale, with_energy)
        on_low = [[None] * 3 for _ in range(4)]
        on_high = [[None] * 3 for _ in range(4)]
        for m in range(4):
            for c in range(3):
                change = forces[(4 + m, c)]
                if m > 0:
                    total = forces[(m, c)]
                    on_low[m][c] = total - change
                    on_high[m][c] = total + change
                else:
                    on_low[m][c] = -change
                    on_high[m][c] = change
        return on_low, on_high, energy


def apply_planes(plane, first, last, load, modulus_at, scale, consume, with_energy=False):
    def flat(modes):
        return tuple(v for mode in modes for v in mode)

    def nested(values):
        return [[values[3 * m + c] for c in range(3)] for m in range(4)]

    def body(q, carry):
        low, pending = nested(carry[:12]), nested(carry[12:])
        high = plane.forward(load(q + 1))
        on_low, on_high, energy = plane.element(low, high, modulus_at(q), scale, with_energy)
        total = [[pending[m][c] + on_low[m][c] for c in range(3)] for m in range(4)]
        consume(q, plane.backward(total), energy)
        return flat(high) + flat(on_high)

    start = flat(plane.forward(load(first)))
    zeros = tuple(jnp.zeros((ROWS, COLS), jnp.float32) for _ in range(12))
    carry = lax.fori_loop(first, last + 1, body, start + zeros, unroll=True)
    return lambda: plane.backward(nested(carry[12:]))


class CoarseBlock:
    def __init__(self, planes):
        self.rows = 2 * planes
        shape = (self.rows, COLS)
        lane = lax.broadcasted_iota(jnp.int32, shape, 1)
        self.row = lax.broadcasted_iota(jnp.int32, shape, 0)
        self.odd_lane = lane % 2 == 1
        ahead = {0: (1, self.row % 2 == 0), 1: (2, self.row < self.rows - 2)}
        behind = {0: (1, self.row % 2 == 1), 1: (2, self.row >= 2)}
        self.ahead = {"y": (0,) + ahead[0], "z": (0,) + ahead[1], "x": (1, 4, lane < COLS - 4)}
        self.behind = {"y": (0,) + behind[0], "z": (0,) + behind[1], "x": (1, 4, lane >= 4)}

    def next(self, v, along):
        axis, by, mask = self.ahead[along]
        return jnp.where(mask, pltpu.roll(v, v.shape[axis] - by, axis), 0.0)

    def prev(self, v, along):
        axis, by, mask = self.behind[along]
        return jnp.where(mask, pltpu.roll(v, by, axis), 0.0)

    def corner_sum(self, v):
        v = v + self.prev(v, "x")
        return v + self.prev(v, "y")

    def apply(self, comps, modulus, scale):
        modes = {}
        for c, v in enumerate(comps):
            parts = {0: v}
            for bit, along in enumerate("xyz"):
                split = {}
                for number, w in parts.items():
                    ahead = self.next(w, along)
                    split[number] = ahead + w
                    split[number + (1 << bit)] = ahead - w
                parts = split
            for number, w in parts.items():
                modes[(number, c)] = w
        forces, _ = weighted_forces(modes, modulus, scale, False)
        result = []
        for c in range(3):
            parts = {number: forces.get((number, c)) for number in range(8)}
            for bit, along in reversed(list(enumerate("xyz"))):
                joined = {}
                for number in range(1 << bit):
                    total, change = parts[number], parts[number + (1 << bit)]
                    if total is None:
                        joined[number] = self.prev(change, along) - change
                    else:
                        joined[number] = (total - change) + self.prev(total + change, along)
                parts = joined
            result.append(parts[0])
        return result


class Groups:
    def __init__(self):
        lane = lax.broadcasted_iota(jnp.int32, (ROWS, COLS), 1)
        row = lax.broadcasted_iota(jnp.int32, (ROWS, COLS), 0)
        self.lane_in, self.row_in = lane % 4, row % 4
        self.lane_bits = [lane % 2 == 1, lane // 2 % 2 == 1]
        self.row_bits = [row % 2 == 1, row // 2 % 2 == 1]

    def over_rows(self, v):
        for bit in range(2):
            by = 1 << bit
            v = v + jnp.where(self.row_bits[bit], pltpu.roll(v, by, 0), pltpu.roll(v, ROWS - by, 0))
        return v

    def over_lanes(self, v):
        for bit in range(2):
            by = 1 << bit
            v = v + jnp.where(self.lane_bits[bit], pltpu.roll(v, by, 1), pltpu.roll(v, COLS - by, 1))
        return v

    def both(self, v):
        return self.over_lanes(self.over_rows(v))


def modulus_of(density):
    return MODULUS_FLOOR + density * density * density * (1.0 - MODULUS_FLOOR)


def flip_matrix():
    row = lax.broadcasted_iota(jnp.int32, (128, 128), 0)
    return (row + lax.broadcasted_iota(jnp.int32, (128, 128), 1) == 127).astype(jnp.float32)


def flipped(stacked):
    return jnp.dot(stacked, flip_matrix(), precision=lax.Precision.HIGHEST, preferred_element_type=jnp.float32)


def both_halves(source, field, k):
    return jnp.concatenate([source[field, k], source[FIELDS + field, k]], axis=1)


def smooth_kernel(
    slabs, info, own, below, above, smooth, coarse, dens_out, free_out, right_out, mod, x, d, w, right, free, left
):
    plane, groups = Plane(1), Groups()
    slab, sweep_count = info[0], info[2]
    has_below = (slab > 0).astype(jnp.float32)
    has_above = (slab < slabs - 1).astype(jnp.float32)

    places = [(below, k, has_below) for k in range(OWN)]
    places += [(own, k, None) for k in range(OWN)]
    places += [(above, k, has_above) for k in range(OWN)]
    turned = flipped(jnp.concatenate([source[DENSITY, k] for source, k, _ in places], axis=0))
    for e, (source, k, inside) in enumerate(places):
        density = jnp.concatenate([source[DENSITY, k], turned[ROWS * e : ROWS * (e + 1)]], axis=1)
        value = modulus_of(density)
        mod[e] = value if inside is None else value * inside
        if source is own:
            dens_out[k] = density
        if e > 0:
            open_node = 1.0 - both_halves(source, FIXED, k)
            free[e - 1] = open_node if inside is None else open_node * inside

    summed = plane.corner_sum(mod[0])
    for q, (source, k, _) in enumerate(places[1:]):
        lower, summed = summed, plane.corner_sum(mod[q + 1])
        scaling = np.float32(row_total()) * (lower + summed)
        inverse = 1.0 / jnp.where(free[q] > 0.0, scaling, 1.0)
        w[q] = inverse
        loaded = free[q] * both_halves(source, LOAD, k)
        right[q] = loaded
        start = loaded * (inverse * np.float32(1.0 / CENTRE))
        for c in range(3):
            x[c, q] = start * np.float32(DIRECTION[c])
            d[c, q] = start * np.float32(DIRECTION[c])

    def load(q):
        f = free[q]
        return [f * x[c, q] for c in range(3)]

    def modulus_at(q):
        return mod[q + 1]

    for k, (keep, add) in enumerate(chebyshev_factors(), 1):

        @pl.when(k < sweep_count)
        def _(k=k, keep=keep, add=add):
            def consume(q, forces, _energy):
                f, weight = free[q], w[q] * np.float32(add)
                is_free = f > 0.0
                loaded = right[q]
                for c in range(3):
                    now = x[c, q]
                    image = jnp.where(is_free, forces[c], now)
                    defect = loaded * np.float32(DIRECTION[c]) - image
                    update = np.float32(keep) * d[c, q] + weight * defect
                    d[c, q] = update
                    x[c, q] = now + update

            apply_planes(plane, k - 1, 10 - k, load, modulus_at, 1.0, consume)

    def consume_left(q, forces, _energy):
        is_free = free[q] > 0.0
        for c in range(3):
            image = jnp.where(is_free, forces[c], x[c, q])
            left[c, q - 3] = right[q] * np.float32(DIRECTION[c]) - image

    rest = apply_planes(plane, 3, 6, load, modulus_at, 1.0, consume_left)()

    odd = groups.lane_bits[0]
    fields = []
    for c in range(3):
        for k in range(5):
            smooth[c, k] = x[c, k + 3]
        mine = groups.both((left[c, 0] + left[c, 1]) + (left[c, 2] + left[c, 3]))
        passed = groups.both(free[7] * -rest[c])
        fields.append(jnp.where(odd, passed, mine))
    fields.append(groups.both((mod[4] + mod[5]) + (mod[6] + mod[7])) * np.float32(1.0 / 64.0))
    for f, field in enumerate(fields):
        coarse[2 * f : 2 * f + 1] = field[0:1]
        coarse[2 * f + 1 : 2 * f + 2] = field[4:5]
    for k in range(5):
        free_out[k] = free[k + 3]
    for k in range(OWN):
        right_out[k] = right[k + 3]


def correct_kernel(
    slabs, info, smooth, dens, free, right, gathered, moved, image, passed, slope, sums, window, d, xc, x, p, own_mod, energy
):
    plane, block = Plane(1), CoarseBlock(8)
    slab, mirror, sweep_count = info[0], info[1], info[3]
    offset = slab % 4
    upper_rows = lax.broadcasted_iota(jnp.int32, (ROWS, COLS), 0) >= 4
    sources = [(k, ROWS) for k in range(4)] + [(k, 0) for k in range(4)] + [(4 + k, ROWS) for k in range(4)]

    for lead in range(4):

        @pl.when(offset == lead)
        def _(lead=lead):
            for q in range(9):
                source, row = sources[lead + q]
                for f in range(4):
                    window[f, 2 * q : 2 * q + 2] = gathered[source, row + 2 * f : row + 2 * f + 2]

    modulus = window[3, 2:18]
    scaling = block.corner_sum(window[3, 0:16]) + block.corner_sum(modulus)
    scaling = np.float32(4.0 * row_total()) * scaling
    at = slab - 3 + block.row // 2
    inside = ((at >= 0) & (at < slabs)).astype(jnp.float32)
    inverse = inside / jnp.where(scaling > 0.0, scaling, 1.0)
    targets = []
    for c in range(3):
        lower, value = window[c, 0:16], window[c, 2:18]
        part = jnp.where(block.odd_lane, pltpu.roll(value, 1, 1), value)
        target = part + jnp.where(block.odd_lane, lower, pltpu.roll(lower, COLS - 1, 1))
        targets.append(target)
        start = target * (inverse * np.float32(1.0 / CENTRE))
        xc[c] = start
        d[c] = start

    for k, (keep, add) in enumerate(chebyshev_factors(), 1):

        @pl.when(k < sweep_count)
        def _(k=k, keep=keep, add=add):
            now = [xc[c] for c in range(3)]
            forces = block.apply(now, modulus, 4.0)
            weight = inverse * np.float32(add)
            for c in range(3):
                update = np.float32(keep) * d[c] + weight * (targets[c] - forces[c])
                d[c] = update
                xc[c] = now[c] + update

    def prolonged(c, q):
        first = jnp.broadcast_to(xc[c, 2 * q : 2 * q + 1], (ROWS, COLS))
        return jnp.where(upper_rows, jnp.broadcast_to(xc[c, 2 * q + 1 : 2 * q + 2], (ROWS, COLS)), first)

    spread = [[prolonged(c, q) for q in (3, 4)] for c in range(3)]
    half = pl.ds(pl.multiple_of(mirror * 128, 128), 128)
    for k in range(5):
        for c in range(3):
            p[c, k] = smooth[c, k] + free[k] * spread[c][1 if k == 4 else 0]
    for k in range(OWN):
        own_mod[k] = modulus_of(dens[k])

    def consume_image(q, forces, strain):
        for c in range(3):
            x[c, q] = forces[c]
        energy[q] = strain

    def load_p(q):
        f = free[q]
        return [f * p[c, q] for c in range(3)]

    rest = apply_planes(plane, 0, 3, load_p, lambda q: own_mod[q], 1.0, consume_image, True)()

    first = jnp.zeros((ROWS, COLS), jnp.float32)
    second = jnp.zeros((ROWS, COLS), jnp.float32)
    for c in range(3):
        x[c, 4] = rest[c]
        passed[c] = x[c, 4, :, half]
    for k in range(OWN):
        second = second + own_mod[k] * energy[k]
        for c in range(3):
            value = p[c, k]
            first = first + (right[k] * np.float32(DIRECTION[c])) * value
            second = second + (1.0 - free[k]) * (value * value)
            moved[c, k] = p[c, k, :, half]
            image[c, k] = x[c, k, :, half]
        density = dens[k]
        energy[k] = np.float32(-3.0 * (1.0 - MODULUS_FLOOR)) * (density * density) * energy[k]
    turned = flipped(jnp.concatenate([energy[k, :, 128:] for k in range(OWN)], axis=0))
    for k in range(OWN):
        slope[k] = energy[k, :, :128] + turned[ROWS * k : ROWS * (k + 1)]
    lane = lax.broadcasted_iota(jnp.int32, (1, 128), 1)
    dots = jnp.where(lane == 0, jnp.sum(first), jnp.where(lane == 1, jnp.sum(second), 0.0))
    for k in range(sums.shape[0]):
        sums[k] = dots


def scale_kernel(totals, load, fixed, moved, image, arrived, slope, displacement, residual, sensitivity):
    total = totals[0]
    for k in range(1, totals.shape[0]):
        total = total + totals[k]
    lane = lax.broadcasted_iota(jnp.int32, (1, 128), 1)
    residual_dot = jnp.sum(jnp.where(lane == 0, total, 0.0), axis=1, keepdims=True)
    curvature = jnp.sum(jnp.where(lane == 1, total, 0.0), axis=1, keepdims=True)
    alpha = jnp.broadcast_to(residual_dot / curvature, (ROWS, 128))
    for k in range(OWN):
        loaded = ((1 - fixed[0, k]) * load[0, k]).astype(jnp.float32)
        for c in range(3):
            displacement[c, k] = alpha * moved[c, k]
            forces = image[c, k] + arrived[c] if k == 0 else image[c, k]
            forces = jnp.where(fixed[0, k] == 0, forces, moved[c, k])
            residual[c, k] = loaded * np.float32(DIRECTION[c]) - alpha * forces
        sensitivity[k] = alpha * (alpha * slope[k])


def call(kernel, outs, ins, scratch=()):
    vmem = pl.BlockSpec(memory_space=pltpu.VMEM)
    smem = pl.BlockSpec(memory_space=pltpu.SMEM)
    return pl.pallas_call(
        kernel,
        out_shape=[jax.ShapeDtypeStruct(shape, jnp.float32) for shape in outs],
        in_specs=[smem if v.ndim == 1 else vmem for v in ins],
        out_specs=[vmem] * len(outs),
        scratch_shapes=[pltpu.VMEM(shape, jnp.float32) for shape in scratch],
        compiler_params=pltpu.CompilerParams(vmem_limit_bytes=16 * 1024 * 1024),
    )(*ins)


def shifted(array, axis, by):
    length = lax.axis_size(axis)
    pairs = [(i, i + by) for i in range(length) if 0 <= i + by < length]
    return lax.ppermute(array, axis, pairs)


def run_smooth(slabs, info, own, below, above):
    plane = (ROWS, COLS)
    field = (3, 11) + plane
    return call(
        functools.partial(smooth_kernel, slabs),
        [(3, 5) + plane, plane, (OWN,) + plane, (5,) + plane, (OWN,) + plane],
        [info, own, below, above],
        [(12,) + plane, field, field, (11,) + plane, (11,) + plane, (11,) + plane, (3, 4) + plane],
    )


def run_correct(slabs, group, info, smooth, dens, free, right, gathered):
    plane = (ROWS, COLS)
    block = (3, 16, COLS)
    part = (3, OWN, ROWS, 128)
    return call(
        functools.partial(correct_kernel, slabs),
        [part, part, (3, ROWS, 128), part[1:], (group, 1, 128)],
        [info, smooth, dens, free, right, gathered],
        [(4, 24, COLS), block, block, (3, 5) + plane, (3, 5) + plane, (OWN,) + plane, (OWN,) + plane],
    )


def on_device(density, load_mask, fixed_mask, sweeps):
    slabs = lax.axis_size(SLAB)
    slab, mirror = lax.axis_index(SLAB), lax.axis_index("mirror")
    info = jnp.concatenate([jnp.stack([slab, mirror]).astype(jnp.int32), sweeps])

    here = jnp.concatenate([density[None], load_mask.astype(jnp.float32), fixed_mask.astype(jnp.float32)], axis=0)
    own = lax.all_gather(here, "mirror").reshape((2 * FIELDS,) + density.shape)
    near = [(i, i + 1) for i in range(slabs - 1)]
    near += [(slabs + i + 1, slabs + i) for i in range(slabs - 1)]
    both = lax.all_gather(lax.ppermute(own, ("mirror",) + SLAB, near), "mirror")
    below, above = both[0], both[1]
    smooth, coarse, dens, free, right = run_smooth(slabs, info, own, below, above)

    reach = 4
    pairs = [(i, i + reach) for i in range(slabs - reach)]
    pairs += [(slabs + i + reach, slabs + i) for i in range(slabs - reach)]
    arrived = lax.ppermute(coarse, ("mirror",) + SLAB, pairs)
    sent = jnp.broadcast_to(jnp.concatenate([coarse, arrived], axis=0), (8, 2 * ROWS, COLS))
    gathered = lax.all_to_all(sent, ("mirror", "x"), 0, 0)

    part = (3, OWN, ROWS, 128)
    group = lax.axis_size(("y", "x"))
    moved, image, passed, slope, sums = run_correct(slabs, group, info, smooth, dens, free, right, gathered)
    added = shifted(passed, SLAB, 1)
    sums = lax.all_to_all(sums, ("y", "x"), 0, 0)
    length = lax.axis_size("z")
    sums = jnp.broadcast_to(jnp.sum(sums, axis=0), (length, 1, 128))
    sums = lax.all_to_all(sums, "z", 0, 0)
    displacement, residual, sensitivity = call(
        scale_kernel, [part, part, part[1:]], [sums, load_mask, fixed_mask, moved, image, added, slope]
    )
    return displacement[None], residual[None], sensitivity


def solution(mesh):
    slabs = mesh.shape["slab"]
    ways = 4
    deep = min(16, slabs // ways)
    split = Mesh(mesh.devices.reshape(2, slabs // (ways * deep), deep, ways), ("mirror",) + SLAB)
    return jax.shard_map(
        on_device,
        mesh=split,
        in_specs=(
            P(SLAB, None, None),
            P("mirror", SLAB, None, None),
            P("mirror", SLAB, None, None),
            P(),
        ),
        out_specs=(
            P("mirror", None, SLAB, None, None),
            P("mirror", None, SLAB, None, None),
            P(SLAB, None, None),
        ),
        check_vma=False,
    )
```

```python
import functools

import jax
import jax.numpy as jnp
import numpy as np
from jax import lax
from jax.experimental import pallas as pl
from jax.experimental.pallas import tpu as pltpu
from jax.sharding import Mesh
from jax.sharding import PartitionSpec as P

SWEEPS = 4
MODULUS_FLOOR = 0.001
EIG_LOWER = 0.05
EIG_UPPER = 1.0
CENTRE = 0.5 * (EIG_UPPER + EIG_LOWER)
HALF_WIDTH = 0.5 * (EIG_UPPER - EIG_LOWER)
DIRECTION = (0.4, -0.3, -1.0)
SLAB = ("y", "z", "x")
ROWS = 8
COLS = 256
OWN = 4
DENSITY, LOAD, FIXED, FIELDS = 0, 1, 2, 3


def element_matrix():
    poisson = 0.3
    lame_first = poisson / ((1.0 + poisson) * (1.0 - 2.0 * poisson))
    shear_modulus = 0.5 / (1.0 + poisson)
    elastic = np.zeros((6, 6))
    elastic[:3, :3] = lame_first
    for i in range(3):
        elastic[i, i] += 2.0 * shear_modulus
        elastic[i + 3, i + 3] = shear_modulus
    points = [0.5 - 0.5 / np.sqrt(3.0), 0.5 + 0.5 / np.sqrt(3.0)]
    stiffness = np.zeros((24, 24))
    for p in points:
        for q in points:
            for s in points:
                strain = np.zeros((6, 24))
                for corner in range(8):
                    z_bit, y_bit, x_bit = (corner // 4, corner // 2 % 2, corner % 2)
                    weight_z = p if z_bit else 1.0 - p
                    weight_y = q if y_bit else 1.0 - q
                    weight_x = s if x_bit else 1.0 - s
                    slope_z = 1.0 if z_bit else -1.0
                    slope_y = 1.0 if y_bit else -1.0
                    slope_x = 1.0 if x_bit else -1.0
                    grad_x = slope_x * weight_y * weight_z
                    grad_y = weight_x * slope_y * weight_z
                    grad_z = weight_x * weight_y * slope_z
                    c = 3 * corner
                    strain[0, c] = grad_x
                    strain[1, c + 1] = grad_y
                    strain[2, c + 2] = grad_z
                    strain[3, c] = grad_y
                    strain[3, c + 1] = grad_x
                    strain[4, c + 1] = grad_z
                    strain[4, c + 2] = grad_y
                    strain[5, c] = grad_z
                    strain[5, c + 2] = grad_x
                stiffness += strain.T @ elastic @ strain / 8.0
    return stiffness


STRETCH = ((1, 0), (2, 1), (4, 2))
SHEAR = (((2, 0), (1, 1)), ((4, 0), (1, 2)), ((4, 1), (2, 2)))
BEND = (((5, 0), (6, 1)), ((3, 0), (6, 2)), ((3, 1), (5, 2)))
TWIST = ((6, 0), (5, 1), (3, 2))
WARP = ((7, 0), (7, 1), (7, 2))


@functools.lru_cache(None)
def mode_entries():
    one = np.array([[1.0, 1.0], [-1.0, 1.0]])
    signs = np.kron(np.kron(one, one), one)
    spread = np.kron(signs, np.eye(3)) / 8.0
    matrix = spread @ element_matrix() @ spread.T

    def at(row, col):
        return matrix[3 * row[0] + row[1], 3 * col[0] + col[1]]

    names = {
        "stretch": (at(STRETCH[0], STRETCH[0]), at(STRETCH[0], STRETCH[1])),
        "shear": at(SHEAR[0][0], SHEAR[0][1]),
        "bend": (at(BEND[0][0], BEND[0][0]), at(BEND[0][0], BEND[0][1])),
        "twist": at(TWIST[0], TWIST[1]),
        "warp": at(WARP[0], WARP[0]),
    }
    again = np.zeros((24, 24))

    def put(modes, diagonal, other):
        for row in modes:
            for col in modes:
                again[3 * row[0] + row[1], 3 * col[0] + col[1]] = diagonal if row == col else other

    put(STRETCH, *names["stretch"])
    put(TWIST, 2.0 * names["twist"], names["twist"])
    for pair in SHEAR:
        put(pair, names["shear"], names["shear"])
    for pair in BEND:
        put(pair, *names["bend"])
    for mode in WARP:
        put((mode,), names["warp"], 0.0)
    assert np.allclose(matrix, again, rtol=0.0, atol=1e-13)
    return names


def mode_forces(modes, scale):
    entries = mode_entries()
    forces = {}
    diagonal, other = entries["stretch"]
    shared = (modes[STRETCH[0]] + modes[STRETCH[1]] + modes[STRETCH[2]]) * np.float32(other * scale)
    for mode in STRETCH:
        forces[mode] = shared + modes[mode] * np.float32((diagonal - other) * scale)
    for first, second in SHEAR:
        forces[first] = forces[second] = (modes[first] + modes[second]) * np.float32(entries["shear"] * scale)
    diagonal, other = np.float32(entries["bend"][0] * scale), np.float32(entries["bend"][1] * scale)
    for first, second in BEND:
        forces[first] = modes[first] * diagonal + modes[second] * other
        forces[second] = modes[second] * diagonal + modes[first] * other
    shared = modes[TWIST[0]] + modes[TWIST[1]] + modes[TWIST[2]]
    for mode in TWIST:
        forces[mode] = (shared + modes[mode]) * np.float32(entries["twist"] * scale)
    for mode in WARP:
        forces[mode] = modes[mode] * np.float32(entries["warp"] * scale)
    return forces


def weighted_forces(modes, modulus, scale, with_energy):
    forces = mode_forces(modes, scale)
    energy = None
    if with_energy:
        terms = [forces[first] * (modes[first] + modes[second]) for first, second in SHEAR]
        paired = [mode for pair in SHEAR for mode in pair]
        terms += [forces[mode] * modes[mode] for mode in forces if mode not in paired]
        for term in terms:
            energy = term if energy is None else energy + term
    for first, second in SHEAR:
        forces[first] = forces[second] = modulus * forces[first]
    for mode in STRETCH + TWIST + WARP + BEND[0] + BEND[1] + BEND[2]:
        forces[mode] = modulus * forces[mode]
    return forces, energy


@functools.lru_cache(None)
def row_total():
    totals = np.abs(element_matrix()).sum(axis=1)
    assert np.allclose(totals, totals[0], rtol=1e-12)
    return float(totals[0])


def chebyshev_factors():
    ratio = CENTRE / HALF_WIDTH
    rho = 1.0 / ratio
    factors = []
    for _ in range(1, SWEEPS):
        rho_next = 1.0 / (2.0 * ratio - rho)
        factors.append((rho_next * rho, 2.0 * rho_next / HALF_WIDTH))
        rho = rho_next
    return factors


def run_sweeps(sweeps, count):
    @pl.when(count >= SWEEPS)
    def _():
        for sweep in sweeps:
            sweep()

    @pl.when(count < SWEEPS)
    def _():
        for k, sweep in enumerate(sweeps, 1):
            pl.when(k < count)(sweep)


class Plane:
    def __init__(self, step):
        lane = lax.broadcasted_iota(jnp.int32, (ROWS, COLS), 1)
        row = lax.broadcasted_iota(jnp.int32, (ROWS, COLS), 0)
        self.step = step
        self.lane_not_last = lane < COLS - step
        self.lane_not_first = lane >= step
        self.row_not_last = row < ROWS - step
        self.row_not_first = row >= step

    def next_x(self, v):
        return jnp.where(self.lane_not_last, pltpu.roll(v, COLS - self.step, 1), 0.0)

    def prev_x(self, v):
        return jnp.where(self.lane_not_first, pltpu.roll(v, self.step, 1), 0.0)

    def next_y(self, v):
        return jnp.where(self.row_not_last, pltpu.roll(v, ROWS - self.step, 0), 0.0)

    def prev_y(self, v):
        return jnp.where(self.row_not_first, pltpu.roll(v, self.step, 0), 0.0)

    def corner_sum(self, v):
        v = v + self.prev_x(v)
        return v + self.prev_y(v)

    def forward(self, comps):
        modes = [[None] * 3 for _ in range(4)]
        for c, v in enumerate(comps):
            ahead = self.next_x(v)
            for x_bit, w in enumerate((ahead + v, ahead - v)):
                above = self.next_y(w)
                modes[x_bit][c] = above + w
                modes[2 + x_bit][c] = above - w
        return modes

    def backward(self, modes):
        comps = []
        for c in range(3):
            along = []
            for x_bit in range(2):
                total, change = modes[x_bit][c], modes[2 + x_bit][c]
                along.append((total - change) + self.prev_y(total + change))
            comps.append((along[0] - along[1]) + self.prev_x(along[0] + along[1]))
        return comps

    def element(self, low, high, modulus, scale, with_energy=False):
        modes = {}
        for m in range(4):
            for c in range(3):
                if m > 0:
                    modes[(m, c)] = high[m][c] + low[m][c]
                modes[(4 + m, c)] = high[m][c] - low[m][c]
        forces, energy = weighted_forces(modes, modulus, scale, with_energy)
        on_low = [[None] * 3 for _ in range(4)]
        on_high = [[None] * 3 for _ in range(4)]
        for m in range(4):
            for c in range(3):
                change = forces[(4 + m, c)]
                if m > 0:
                    total = forces[(m, c)]
                    on_low[m][c] = total - change
                    on_high[m][c] = total + change
                else:
                    on_low[m][c] = -change
                    on_high[m][c] = change
        return on_low, on_high, energy


def apply_planes(plane, first, last, load, modulus_at, scale, consume, with_energy=False):
    def flat(modes):
        return tuple(v for mode in modes for v in mode)

    def nested(values):
        return [[values[3 * m + c] for c in range(3)] for m in range(4)]

    def body(q, carry):
        low, pending = nested(carry[:12]), nested(carry[12:])
        high = plane.forward(load(q + 1))
        on_low, on_high, energy = plane.element(low, high, modulus_at(q), scale, with_energy)
        total = [[pending[m][c] + on_low[m][c] for c in range(3)] for m in range(4)]
        consume(q, plane.backward(total), energy)
        return flat(high) + flat(on_high)

    start = flat(plane.forward(load(first)))
    zeros = tuple(jnp.zeros((ROWS, COLS), jnp.float32) for _ in range(12))
    carry = lax.fori_loop(first, last + 1, body, start + zeros, unroll=True)
    return lambda: plane.backward(nested(carry[12:]))


class CoarseBlock:
    def __init__(self, planes):
        self.rows = 2 * planes
        shape = (self.rows, COLS)
        lane = lax.broadcasted_iota(jnp.int32, shape, 1)
        self.row = lax.broadcasted_iota(jnp.int32, shape, 0)
        self.odd_lane = lane % 2 == 1
        ahead = {0: (1, self.row % 2 == 0), 1: (2, self.row < self.rows - 2)}
        behind = {0: (1, self.row % 2 == 1), 1: (2, self.row >= 2)}
        self.ahead = {"y": (0,) + ahead[0], "z": (0,) + ahead[1], "x": (1, 4, lane < COLS - 4)}
        self.behind = {"y": (0,) + behind[0], "z": (0,) + behind[1], "x": (1, 4, lane >= 4)}

    def next(self, v, along):
        axis, by, mask = self.ahead[along]
        return jnp.where(mask, pltpu.roll(v, v.shape[axis] - by, axis), 0.0)

    def prev(self, v, along):
        axis, by, mask = self.behind[along]
        return jnp.where(mask, pltpu.roll(v, by, axis), 0.0)

    def corner_sum(self, v):
        v = v + self.prev(v, "x")
        return v + self.prev(v, "y")

    def apply(self, comps, modulus, scale):
        modes = {}
        for c, v in enumerate(comps):
            parts = {0: v}
            for bit, along in enumerate("xyz"):
                split = {}
                for number, w in parts.items():
                    ahead = self.next(w, along)
                    split[number] = ahead + w
                    split[number + (1 << bit)] = ahead - w
                parts = split
            for number, w in parts.items():
                modes[(number, c)] = w
        forces, _ = weighted_forces(modes, modulus, scale, False)
        result = []
        for c in range(3):
            parts = {number: forces.get((number, c)) for number in range(8)}
            for bit, along in reversed(list(enumerate("xyz"))):
                joined = {}
                for number in range(1 << bit):
                    total, change = parts[number], parts[number + (1 << bit)]
                    if total is None:
                        joined[number] = self.prev(change, along) - change
                    else:
                        joined[number] = (total - change) + self.prev(total + change, along)
                parts = joined
            result.append(parts[0])
        return result


class Groups:
    def __init__(self):
        lane = lax.broadcasted_iota(jnp.int32, (ROWS, COLS), 1)
        row = lax.broadcasted_iota(jnp.int32, (ROWS, COLS), 0)
        self.lane_in, self.row_in = lane % 4, row % 4
        self.lane_bits = [lane % 2 == 1, lane // 2 % 2 == 1]
        self.row_bits = [row % 2 == 1, row // 2 % 2 == 1]

    def over_rows(self, v):
        for bit in range(2):
            by = 1 << bit
            v = v + jnp.where(self.row_bits[bit], pltpu.roll(v, by, 0), pltpu.roll(v, ROWS - by, 0))
        return v

    def over_lanes(self, v):
        for bit in range(2):
            by = 1 << bit
            v = v + jnp.where(self.lane_bits[bit], pltpu.roll(v, by, 1), pltpu.roll(v, COLS - by, 1))
        return v

    def both(self, v):
        return self.over_lanes(self.over_rows(v))


def modulus_of(density):
    return MODULUS_FLOOR + density * density * density * (1.0 - MODULUS_FLOOR)


def flip_matrix():
    row = lax.broadcasted_iota(jnp.int32, (128, 128), 0)
    return (row + lax.broadcasted_iota(jnp.int32, (128, 128), 1) == 127).astype(jnp.float32)


def flipped(stacked):
    return jnp.dot(stacked, flip_matrix(), precision=lax.Precision.HIGHEST, preferred_element_type=jnp.float32)


def both_halves(source, field, k):
    return jnp.concatenate([source[field, k], source[FIELDS + field, k]], axis=1)


def smooth_kernel(
    slabs, info, own, below, above, smooth, coarse, dens_out, free_out, right_out, mod, x, d, w, right, free, left
):
    plane, groups = Plane(1), Groups()
    slab, sweep_count = info[0], info[2]
    has_below = (slab > 0).astype(jnp.float32)
    has_above = (slab < slabs - 1).astype(jnp.float32)

    places = [(below, k, has_below) for k in range(OWN)]
    places += [(own, k, None) for k in range(OWN)]
    places += [(above, k, has_above) for k in range(OWN)]
    turned = flipped(jnp.concatenate([source[DENSITY, k] for source, k, _ in places], axis=0))
    for e, (source, k, inside) in enumerate(places):
        density = jnp.concatenate([source[DENSITY, k], turned[ROWS * e : ROWS * (e + 1)]], axis=1)
        value = modulus_of(density)
        mod[e] = value if inside is None else value * inside
        if source is own:
            dens_out[k] = density
        if e > 0:
            open_node = 1.0 - both_halves(source, FIXED, k)
            free[e - 1] = open_node if inside is None else open_node * inside

    summed = plane.corner_sum(mod[0])
    for q, (source, k, _) in enumerate(places[1:]):
        lower, summed = summed, plane.corner_sum(mod[q + 1])
        scaling = np.float32(row_total()) * (lower + summed)
        inverse = 1.0 / jnp.where(free[q] > 0.0, scaling, 1.0)
        w[q] = inverse
        loaded = free[q] * both_halves(source, LOAD, k)
        right[q] = loaded
        start = loaded * (inverse * np.float32(1.0 / CENTRE))
        for c in range(3):
            x[c, q] = start * np.float32(DIRECTION[c])
            d[c, q] = start * np.float32(DIRECTION[c])

    def load(q):
        f = free[q]
        return [f * x[c, q] for c in range(3)]

    def modulus_at(q):
        return mod[q + 1]

    sweeps = []
    for k, (keep, add) in enumerate(chebyshev_factors(), 1):

        def sweep(k=k, keep=keep, add=add):
            def consume(q, forces, _energy):
                f, weight = free[q], w[q] * np.float32(add)
                is_free = f > 0.0
                loaded = right[q]
                for c in range(3):
                    now = x[c, q]
                    image = jnp.where(is_free, forces[c], now)
                    defect = loaded * np.float32(DIRECTION[c]) - image
                    update = np.float32(keep) * d[c, q] + weight * defect
                    d[c, q] = update
                    x[c, q] = now + update

            apply_planes(plane, k - 1, 10 - k, load, modulus_at, 1.0, consume)

        sweeps.append(sweep)

    run_sweeps(sweeps, sweep_count)

    def consume_left(q, forces, _energy):
        is_free = free[q] > 0.0
        for c in range(3):
            image = jnp.where(is_free, forces[c], x[c, q])
            left[c, q - 3] = right[q] * np.float32(DIRECTION[c]) - image

    rest = apply_planes(plane, 3, 6, load, modulus_at, 1.0, consume_left)()

    odd = groups.lane_bits[0]
    fields = []
    for c in range(3):
        for k in range(5):
            smooth[c, k] = x[c, k + 3]
        mine = groups.both((left[c, 0] + left[c, 1]) + (left[c, 2] + left[c, 3]))
        passed = groups.both(free[7] * -rest[c])
        fields.append(jnp.where(odd, passed, mine))
    fields.append(groups.both((mod[4] + mod[5]) + (mod[6] + mod[7])) * np.float32(1.0 / 64.0))
    for f, field in enumerate(fields):
        coarse[2 * f : 2 * f + 1] = field[0:1]
        coarse[2 * f + 1 : 2 * f + 2] = field[4:5]
    for k in range(5):
        free_out[k] = free[k + 3]
    for k in range(OWN):
        right_out[k] = right[k + 3]


def correct_kernel(
    slabs, info, smooth, dens, free, right, gathered, moved, image, passed, slope, sums, window, d, xc, x, p, own_mod, energy
):
    plane, block = Plane(1), CoarseBlock(8)
    slab, mirror, sweep_count = info[0], info[1], info[3]
    offset = slab % 4
    upper_rows = lax.broadcasted_iota(jnp.int32, (ROWS, COLS), 0) >= 4
    sources = [(k, ROWS) for k in range(4)] + [(k, 0) for k in range(4)] + [(4 + k, ROWS) for k in range(4)]

    for lead in range(4):

        @pl.when(offset == lead)
        def _(lead=lead):
            for q in range(9):
                source, row = sources[lead + q]
                for f in range(4):
                    window[f, 2 * q : 2 * q + 2] = gathered[source, row + 2 * f : row + 2 * f + 2]

    modulus = window[3, 2:18]
    scaling = block.corner_sum(window[3, 0:16]) + block.corner_sum(modulus)
    scaling = np.float32(4.0 * row_total()) * scaling
    at = slab - 3 + block.row // 2
    inside = ((at >= 0) & (at < slabs)).astype(jnp.float32)
    inverse = inside / jnp.where(scaling > 0.0, scaling, 1.0)
    targets = []
    for c in range(3):
        lower, value = window[c, 0:16], window[c, 2:18]
        part = jnp.where(block.odd_lane, pltpu.roll(value, 1, 1), value)
        target = part + jnp.where(block.odd_lane, lower, pltpu.roll(lower, COLS - 1, 1))
        targets.append(target)
        start = target * (inverse * np.float32(1.0 / CENTRE))
        xc[c] = start
        d[c] = start

    sweeps = []
    for k, (keep, add) in enumerate(chebyshev_factors(), 1):

        def sweep(k=k, keep=keep, add=add):
            now = [xc[c] for c in range(3)]
            forces = block.apply(now, modulus, 4.0)
            weight = inverse * np.float32(add)
            for c in range(3):
                update = np.float32(keep) * d[c] + weight * (targets[c] - forces[c])
                d[c] = update
                xc[c] = now[c] + update

        sweeps.append(sweep)

    run_sweeps(sweeps, sweep_count)

    def prolonged(c, q):
        first = jnp.broadcast_to(xc[c, 2 * q : 2 * q + 1], (ROWS, COLS))
        return jnp.where(upper_rows, jnp.broadcast_to(xc[c, 2 * q + 1 : 2 * q + 2], (ROWS, COLS)), first)

    spread = [[prolonged(c, q) for q in (3, 4)] for c in range(3)]
    half = pl.ds(pl.multiple_of(mirror * 128, 128), 128)
    for k in range(5):
        for c in range(3):
            p[c, k] = smooth[c, k] + free[k] * spread[c][1 if k == 4 else 0]
    for k in range(OWN):
        own_mod[k] = modulus_of(dens[k])

    def consume_image(q, forces, strain):
        for c in range(3):
            x[c, q] = forces[c]
        energy[q] = strain

    def load_p(q):
        f = free[q]
        return [f * p[c, q] for c in range(3)]

    rest = apply_planes(plane, 0, 3, load_p, lambda q: own_mod[q], 1.0, consume_image, True)()

    first = jnp.zeros((ROWS, COLS), jnp.float32)
    second = jnp.zeros((ROWS, COLS), jnp.float32)
    for c in range(3):
        x[c, 4] = rest[c]
        passed[c] = x[c, 4, :, half]
    for k in range(OWN):
        second = second + own_mod[k] * energy[k]
        for c in range(3):
            value = p[c, k]
            first = first + (right[k] * np.float32(DIRECTION[c])) * value
            second = second + (1.0 - free[k]) * (value * value)
            moved[c, k] = p[c, k, :, half]
            image[c, k] = x[c, k, :, half]
        density = dens[k]
        energy[k] = np.float32(-3.0 * (1.0 - MODULUS_FLOOR)) * (density * density) * energy[k]
    turned = flipped(jnp.concatenate([energy[k, :, 128:] for k in range(OWN)], axis=0))
    for k in range(OWN):
        slope[k] = energy[k, :, :128] + turned[ROWS * k : ROWS * (k + 1)]
    lane = lax.broadcasted_iota(jnp.int32, (1, 128), 1)
    dots = jnp.where(lane == 0, jnp.sum(first), jnp.where(lane == 1, jnp.sum(second), 0.0))
    for k in range(sums.shape[0]):
        sums[k] = dots


def scale_kernel(totals, load, fixed, moved, image, arrived, slope, displacement, residual, sensitivity):
    total = totals[0]
    for k in range(1, totals.shape[0]):
        total = total + totals[k]
    lane = lax.broadcasted_iota(jnp.int32, (1, 128), 1)
    residual_dot = jnp.sum(jnp.where(lane == 0, total, 0.0), axis=1, keepdims=True)
    curvature = jnp.sum(jnp.where(lane == 1, total, 0.0), axis=1, keepdims=True)
    alpha = jnp.broadcast_to(residual_dot / curvature, (ROWS, 128))
    for k in range(OWN):
        loaded = ((1 - fixed[0, k]) * load[0, k]).astype(jnp.float32)
        for c in range(3):
            displacement[c, k] = alpha * moved[c, k]
            forces = image[c, k] + arrived[c] if k == 0 else image[c, k]
            forces = jnp.where(fixed[0, k] == 0, forces, moved[c, k])
            residual[c, k] = loaded * np.float32(DIRECTION[c]) - alpha * forces
        sensitivity[k] = alpha * (alpha * slope[k])


def call(kernel, outs, ins, scratch=()):
    vmem = pl.BlockSpec(memory_space=pltpu.VMEM)
    smem = pl.BlockSpec(memory_space=pltpu.SMEM)
    return pl.pallas_call(
        kernel,
        out_shape=[jax.ShapeDtypeStruct(shape, jnp.float32) for shape in outs],
        in_specs=[smem if v.ndim == 1 else vmem for v in ins],
        out_specs=[vmem] * len(outs),
        scratch_shapes=[pltpu.VMEM(shape, jnp.float32) for shape in scratch],
        compiler_params=pltpu.CompilerParams(vmem_limit_bytes=16 * 1024 * 1024),
    )(*ins)


def shifted(array, axis, by):
    length = lax.axis_size(axis)
    pairs = [(i, i + by) for i in range(length) if 0 <= i + by < length]
    return lax.ppermute(array, axis, pairs)


def run_smooth(slabs, info, own, below, above):
    plane = (ROWS, COLS)
    field = (3, 11) + plane
    return call(
        functools.partial(smooth_kernel, slabs),
        [(3, 5) + plane, plane, (OWN,) + plane, (5,) + plane, (OWN,) + plane],
        [info, own, below, above],
        [(12,) + plane, field, field, (11,) + plane, (11,) + plane, (11,) + plane, (3, 4) + plane],
    )


def run_correct(slabs, group, info, smooth, dens, free, right, gathered):
    plane = (ROWS, COLS)
    block = (3, 16, COLS)
    part = (3, OWN, ROWS, 128)
    return call(
        functools.partial(correct_kernel, slabs),
        [part, part, (3, ROWS, 128), part[1:], (group, 1, 128)],
        [info, smooth, dens, free, right, gathered],
        [(4, 24, COLS), block, block, (3, 5) + plane, (3, 5) + plane, (OWN,) + plane, (OWN,) + plane],
    )


def on_device(density, load_mask, fixed_mask, sweeps):
    slabs = lax.axis_size(SLAB)
    slab, mirror = lax.axis_index(SLAB), lax.axis_index("mirror")
    info = jnp.concatenate([jnp.stack([slab, mirror]).astype(jnp.int32), sweeps])

    here = jnp.concatenate([density[None], load_mask.astype(jnp.float32), fixed_mask.astype(jnp.float32)], axis=0)
    own = lax.all_gather(here, "mirror").reshape((2 * FIELDS,) + density.shape)
    near = [(i, i + 1) for i in range(slabs - 1)]
    near += [(slabs + i + 1, slabs + i) for i in range(slabs - 1)]
    both = lax.all_gather(lax.ppermute(own, ("mirror",) + SLAB, near), "mirror")
    below, above = both[0], both[1]
    smooth, coarse, dens, free, right = run_smooth(slabs, info, own, below, above)

    reach = 4
    pairs = [(i, i + reach) for i in range(slabs - reach)]
    pairs += [(slabs + i + reach, slabs + i) for i in range(slabs - reach)]
    arrived = lax.ppermute(coarse, ("mirror",) + SLAB, pairs)
    sent = jnp.broadcast_to(jnp.concatenate([coarse, arrived], axis=0), (8, 2 * ROWS, COLS))
    gathered = lax.all_to_all(sent, ("mirror", "x"), 0, 0)

    part = (3, OWN, ROWS, 128)
    group = lax.axis_size(("y", "x"))
    moved, image, passed, slope, sums = run_correct(slabs, group, info, smooth, dens, free, right, gathered)
    added = shifted(passed, SLAB, 1)
    sums = lax.all_to_all(sums, ("y", "x"), 0, 0)
    length = lax.axis_size("z")
    sums = jnp.broadcast_to(jnp.sum(sums, axis=0), (length, 1, 128))
    sums = lax.all_to_all(sums, "z", 0, 0)
    displacement, residual, sensitivity = call(
        scale_kernel, [part, part, part[1:]], [sums, load_mask, fixed_mask, moved, image, added, slope]
    )
    return displacement[None], residual[None], sensitivity


def solution(mesh):
    slabs = mesh.shape["slab"]
    ways = 4
    deep = min(16, slabs // ways)
    split = Mesh(mesh.devices.reshape(2, slabs // (ways * deep), deep, ways), ("mirror",) + SLAB)
    return jax.shard_map(
        on_device,
        mesh=split,
        in_specs=(
            P(SLAB, None, None),
            P("mirror", SLAB, None, None),
            P("mirror", SLAB, None, None),
            P(),
        ),
        out_specs=(
            P("mirror", None, SLAB, None, None),
            P("mirror", None, SLAB, None, None),
            P(SLAB, None, None),
        ),
        check_vma=False,
    )
```
